256 devices in a mesh: chan: 16 (over z, y_hi), patch: 16 (over x, y_lo, core).
Axes of the slice: x: 4, y: 4 (y_hi: 2, y_lo: 2; y = y_hi * 2 + y_lo), z: 8, core: 2. Of those that a mesh axis runs over, the one named last changes fastest.
Arguments:
- tokens: bfloat16 [64, 3072, 1024], P('chan', 'patch'), may hold values from -6 to 6
- table: int32 [64], P('chan'), may hold values from 0 to 1, as said below
- w_key: bfloat16 [1024, 1024], replicated, may hold values from -0.1875 to 0.1875
- w_value: bfloat16 [1024, 1024], replicated, may hold values from -0.1875 to 0.1875
- query_one: float32 [1024], replicated, may hold values from -100 to 100
- w_key_two: bfloat16 [1024, 1024], replicated, may hold values from -0.1875 to 0.1875
- query_two: float32 [1024], replicated, may hold values from -100 to 100
- cotangent: bfloat16 [16, 192, 1024], P('patch', 'chan'), may hold values from -6 to 6
Outputs:
- token_grad: bfloat16 [64, 3072, 1024], P('chan', 'patch')
- grad_w_key: float32 [1024, 1024], P('patch')
- grad_w_value: float32 [1024, 1024], P('patch')
- grad_w_key_two: float32 [1024, 1024], P('patch')
- grad_query_one: float32 [1024], replicated
- grad_query_two: float32 [1024], replicated
The draws below stay inside these ranges and needn't reach their ends.
Inputs may be any that keep to these rules, and one draw needn't show every extreme that they name: `table`: in every aligned block of 4 channels each of the 2 group numbers appears at least once.
All inputs are finite; a program needn't handle non-finite values.
Results may differ from the reference program's by a relative error of at most 0.0087.
Values may be sent and summed in bfloat16 or wider, within the bound.
No kernel may reach another device: no remote copies, remote signals or barrier semaphores. Data moves between devices by JAX's collectives and lax.ppermute only.
A program may use at most 128 MiB of HBM per device.

```python
import math
import jax
import jax.numpy as jnp
from jax import lax

D = 1024
HEADS = 16
HD = 64
V_DEV = 4
GPD = 2
P_DEV = 192
VARS = 64
GROUPS = 32
PATCHES = 3072
N_PATCH = 16


def draw_table(key, part):
    key = jax.random.fold_in(key, 11)
    key_perm, key_rand = jax.random.split(key)
    blocks = VARS // V_DEV
    perms = jax.vmap(lambda k: jax.random.permutation(k, V_DEV))(jax.random.split(key_perm, blocks))
    inverse = jnp.argsort(perms, axis=1, stable=True).astype(jnp.int32)
    spare = jax.random.randint(key_rand, (blocks, V_DEV), 0, GPD)
    labels = jnp.where(inverse < GPD, inverse, spare)
    return labels.reshape(VARS).astype(jnp.int32)


def draw_query_one(key, part):
    key = jax.random.fold_in(key, 23)
    key_norm = jax.random.fold_in(key, 0)
    base = jax.random.normal(key_norm, (D,), jnp.float32)
    return jnp.clip(base * 1.5, -9.0, 9.0)


def draw_query_two(key, part):
    key = jax.random.fold_in(key, 37)
    key_norm = jax.random.fold_in(key, 0)
    base = jax.random.normal(key_norm, (D,), jnp.float32)
    return jnp.clip(base * 1.5, -9.0, 9.0)


def shard_levels(stream_key, shape, shards, smallest, high):
    gain = 1.0
    for position, parts in shards:
        draws = jax.random.uniform(jax.random.fold_in(jax.random.fold_in(stream_key, 6), position), (parts,), jnp.float32, smallest / len(shards), high / len(shards))
        gain = gain * jnp.repeat(jnp.exp(draws), shape[position] // parts).reshape((-1,) + (1,) * (len(shape) - 1 - position))
    return gain


def centred(stream_key, dims, deviation, reach, shards=(), held_as=jnp.bfloat16):
    values = deviation * jax.random.normal(stream_key, dims, jnp.float32)
    if shards:
        values = values * shard_levels(stream_key, dims, shards, -0.22, 0.18)
    return jnp.clip(values, -reach, reach).astype(held_as)


def setup_inputs(seed: int = 0) -> dict:
    seeds = jax.random.split(jax.random.key(seed), 9)
    tokens = centred(seeds[0], (VARS, PATCHES, D), 1.0, 6.0, ((0, 16), (1, 16)))
    table = draw_table(jax.random.fold_in(seeds[8], 71), 0)
    w_key = centred(seeds[2], (D, D), D ** -0.5, 0.1875)
    w_value = centred(seeds[3], (D, D), D ** -0.5, 0.1875)
    query_one = draw_query_one(jax.random.fold_in(seeds[8], 71), 0)
    w_key_two = centred(seeds[5], (D, D), D ** -0.5, 0.1875)
    query_two = draw_query_two(jax.random.fold_in(seeds[8], 71), 0)
    cotangent = centred(seeds[7], (N_PATCH, P_DEV, D), 1.0, 6.0, ((0, 16), (1, 16)))
    return {"tokens": tokens, "table": table, "w_key": w_key, "w_value": w_value, "query_one": query_one, "w_key_two": w_key_two, "query_two": query_two, "cotangent": cotangent}


def dot_first(left, right):
    return lax.dot_general(left, right, (((0,), (0,)), ((), ())), preferred_element_type=jnp.float32)

def dot_second(left, right):
    return lax.dot_general(left, right, (((1,), (1,)), ((), ())), preferred_element_type=jnp.float32)

def level_one(tokens, onehot, w_key, w_value, query_one):
    chans, rows, width = tokens.shape
    scale_one = 1.0 / math.sqrt(HD)
    flat = tokens.reshape(chans * rows, width)
    keys = jnp.dot(flat, w_key, preferred_element_type=jnp.float32).reshape(chans, rows, HEADS, HD)
    values = jnp.dot(flat, w_value, preferred_element_type=jnp.float32).reshape(chans, rows, HEADS, HD)
    scores = lax.optimization_barrier(jnp.sum(keys * query_one.reshape(HEADS, HD), -1)) * scale_one
    masked = jnp.where(onehot.T[:, :, None, None] > 0, scores[None], -jnp.inf)
    top = lax.optimization_barrier(jnp.max(masked, 1))
    high = lax.Precision.HIGHEST
    chan_top = jnp.einsum('cg,gbh->cbh', onehot, top, precision=high)
    expo = jnp.exp(scores - chan_top)
    total = jnp.einsum('cg,cbh->gbh', onehot, expo, precision=high)
    weights = expo / jnp.einsum('cg,gbh->cbh', onehot, total, precision=high)
    agg = jnp.einsum('cg,cbhk->gbhk', onehot, weights[..., None] * values, precision=high)
    agg = agg.reshape(onehot.shape[1], rows, width).astype(jnp.bfloat16)
    return (agg, keys, values, weights)

def level_one_back(tokens, onehot, w_key, w_value, query_one, keys, values, weights, agg_grad):
    chans, rows, width = tokens.shape
    scale_one = 1.0 / math.sqrt(HD)
    high = lax.Precision.HIGHEST
    agg_f = agg_grad.astype(jnp.float32).reshape(onehot.shape[1], rows, HEADS, HD)
    chan_grad = jnp.einsum('cg,gbhk->cbhk', onehot, agg_f, precision=high)
    value_grad = (weights[..., None] * chan_grad).reshape(chans * rows, width).astype(jnp.bfloat16)
    dw_one = lax.optimization_barrier(jnp.sum(chan_grad * values, -1))
    group_inner = jnp.einsum('cg,cbh->gbh', onehot, weights * dw_one, precision=high)
    score_grad = weights * (dw_one - jnp.einsum('cg,gbh->cbh', onehot, group_inner, precision=high))
    key_grad = (score_grad[..., None] * query_one.reshape(HEADS, HD) * scale_one).reshape(chans * rows, width).astype(jnp.bfloat16)
    query_grad = lax.optimization_barrier(jnp.sum(score_grad[..., None] * keys, (0, 1))).reshape(width) * scale_one
    token_grad = (dot_second(key_grad, w_key) + dot_second(value_grad, w_value)).astype(jnp.bfloat16)
    return (token_grad.reshape(chans, rows, width), tokens.reshape(chans * rows, width), key_grad, value_grad, query_grad)

def level_two_scores(agg, w_key_two, query_two):
    groups, rows, width = agg.shape
    keys_two = jnp.dot(agg.reshape(groups * rows, width), w_key_two, preferred_element_type=jnp.float32)
    keys_two = keys_two.reshape(groups, rows, HEADS, HD)
    scores_two = lax.optimization_barrier(jnp.sum(keys_two * query_two.reshape(HEADS, HD), -1)) * (1.0 / math.sqrt(HD))
    return (keys_two, scores_two)

def cot_products(agg, cot_f):
    groups, rows, width = agg.shape
    return lax.optimization_barrier(jnp.sum(cot_f[None] * agg.astype(jnp.float32).reshape(groups, rows, HEADS, HD), -1))

def level_two_back(agg, keys_two, weights_two, inner_two, dw_two, cot_f, w_key_two, query_two):
    groups, rows, width = agg.shape
    scale_one = 1.0 / math.sqrt(HD)
    value_part = (weights_two[..., None] * cot_f[None]).reshape(groups * rows, width)
    score_grad = weights_two * (dw_two - inner_two[None])
    key_grad = (score_grad[..., None] * query_two.reshape(HEADS, HD) * scale_one).reshape(groups * rows, width).astype(jnp.bfloat16)
    agg_grad = (value_part + dot_second(key_grad, w_key_two)).astype(jnp.bfloat16).reshape(groups, rows, width)
    query_grad = lax.optimization_barrier(jnp.sum(score_grad[..., None] * keys_two, (0, 1))).reshape(width) * scale_one
    return (agg_grad, key_grad, query_grad)

def reference(tokens, table, w_key, w_value, query_one, w_key_two, query_two, cotangent):
    chan_ids = jnp.arange(VARS, dtype=jnp.int32)
    group_ids = chan_ids // V_DEV * GPD + table.astype(jnp.int32)
    onehot = (group_ids[:, None] == jnp.arange(GROUPS, dtype=jnp.int32)[None]).astype(jnp.float32)
    cot_rows = cotangent.reshape(PATCHES, D)

    def advance(block, carry):
        grads, sums, qsum_one, qsum_two = carry
        start = (block * P_DEV).astype(jnp.int32)
        window = lax.dynamic_slice_in_dim(tokens, start, P_DEV, 1)
        cot_f = lax.dynamic_slice_in_dim(cot_rows, start, P_DEV, 0).astype(jnp.float32).reshape(P_DEV, HEADS, HD)
        agg, keys, values, weights = level_one(window, onehot, w_key, w_value, query_one)
        keys_two, scores_two = level_two_scores(agg, w_key_two, query_two)
        expo = jnp.exp(scores_two - lax.optimization_barrier(jnp.max(scores_two, 0)))
        weights_two = expo / lax.optimization_barrier(jnp.sum(expo, 0))
        dw_two = cot_products(agg, cot_f)
        inner_two = lax.optimization_barrier(jnp.sum(weights_two * dw_two, 0))
        agg_grad, key_grad_two, qg_two = level_two_back(agg, keys_two, weights_two, inner_two, dw_two, cot_f, w_key_two, query_two)
        token_grad, flat, key_grad, value_grad, qg_one = level_one_back(window, onehot, w_key, w_value, query_one, keys, values, weights, agg_grad)
        part = jnp.concatenate([dot_first(flat, key_grad), dot_first(flat, value_grad), dot_first(agg.reshape(-1, D), key_grad_two)], 1)
        grads = lax.dynamic_update_slice_in_dim(grads, token_grad, start, 1)
        return (grads, sums + part, qsum_one + qg_one, qsum_two + qg_two)
    init = (jnp.zeros((VARS, PATCHES, D), jnp.bfloat16), jnp.zeros((D, 3 * D), jnp.float32), jnp.zeros((D,), jnp.float32), jnp.zeros((D,), jnp.float32))
    grads, sums, qsum_one, qsum_two = lax.fori_loop(0, N_PATCH, advance, init)
    return (grads, sums[:, :D], sums[:, D:2 * D], sums[:, 2 * D:], qsum_one, qsum_two)
```

```python
import functools

import jax
import jax.numpy as jnp
from jax import lax
from jax.experimental import pallas as pl
from jax.experimental.pallas import tpu as pltpu
from jax.sharding import PartitionSpec as P

D = 1024
HEADS = 16
HD = 64
SHIFT = 6
SCALE = 0.125
CH = 4
GR = 2
ROWS = 192
BLK = 64
NB = ROWS // BLK
TOK = CH * BLK
AGG = GR * BLK
SLAB = 72
F32 = jnp.float32
BF16 = jnp.bfloat16
LIMIT = 40 * 2**20


def nn(a, b):
    return lax.dot_general(a, b, (((1,), (0,)), ((), ())), preferred_element_type=F32)


def nt(a, b):
    return lax.dot_general(a, b, (((1,), (1,)), ((), ())), preferred_element_type=F32)


def split2(x):
    high = x.astype(BF16)
    return high, (x - high.astype(F32)).astype(BF16)


def split3(x):
    high = x.astype(BF16)
    rest = x - high.astype(F32)
    middle = rest.astype(BF16)
    return high, middle, (rest - middle.astype(F32)).astype(BF16)


def spread(copies):
    row = lax.broadcasted_iota(jnp.int32, (copies * HEADS, D), 0) & (HEADS - 1)
    col = lax.broadcasted_iota(jnp.int32, (copies * HEADS, D), 1) >> SHIFT
    return jnp.where(row == col, 1.0, 0.0).astype(BF16)


def expand(x, heads2):
    return nn(jnp.concatenate(split2(x), 1), heads2)


def head_sum(x, heads):
    high, low = split2(x)
    return nt(high, heads) + nt(low, heads)


def fold(weight, query):
    parts = [p.astype(F32) for p in split3(query * SCALE)]
    row = lax.broadcasted_iota(jnp.int32, (HEADS, D), 0)
    col = lax.broadcasted_iota(jnp.int32, (HEADS, D), 1) >> SHIFT
    wide = [jnp.where(row == col, p, 0.0).astype(BF16) for p in parts]
    out = nt(weight, jnp.concatenate(wide, 0))
    total = out[:, :HEADS] + out[:, HEADS : 2 * HEADS] + out[:, 2 * HEADS :]
    return jnp.concatenate(split3(total), 1)


def folded_dot(x, folded):
    out = nn(x, folded)
    return out[:, :HEADS] + out[:, HEADS : 2 * HEADS] + out[:, 2 * HEADS :]


def folded_back(x, folded):
    high, low = split2(x)
    right = jnp.concatenate(
        [folded[:, :HEADS], folded[:, HEADS : 2 * HEADS], folded[:, :HEADS]], 1
    )
    return nt(jnp.concatenate([high, high, low], 1), right)


def forward_kernel(
    table, tok, w_value, w_key, w_key_two, query_one, query_two,
    values, weights, agg, agg_t, tok_t, scores_two, fold_one, fold_two,
):
    @pl.when(pl.program_id(0) == 0)
    def _():
        fold_one[...] = fold(w_key[...], query_one[...])
        fold_two[...] = fold(w_key_two[...], query_two[...])

    flat = tok[...].reshape(TOK, D)
    tok_t[...] = flat.T
    scores = folded_dot(flat, fold_one[...])
    vals = nn(flat, w_value[...])
    values[...] = vals
    group = [table[c] for c in range(CH)]
    score = [scores[c * BLK : (c + 1) * BLK] for c in range(CH)]
    top = [
        functools.reduce(
            jnp.maximum, [jnp.where(group[c] == g, score[c], -jnp.inf) for c in range(CH)]
        )
        for g in range(GR)
    ]
    expo = [jnp.exp(score[c] - jnp.where(group[c] == 0, top[0], top[1])) for c in range(CH)]
    total = [sum(jnp.where(group[c] == g, expo[c], 0.0) for c in range(CH)) for g in range(GR)]
    weight = jnp.concatenate(
        [expo[c] / jnp.where(group[c] == 0, total[0], total[1]) for c in range(CH)], 0
    )
    weights[...] = weight
    mixed = expand(weight, spread(2)) * vals
    part = [mixed[c * BLK : (c + 1) * BLK] for c in range(CH)]
    both = jnp.concatenate(
        [sum(jnp.where(group[c] == g, part[c], 0.0) for c in range(CH)) for g in range(GR)], 0
    ).astype(BF16)
    agg[...] = both
    agg_t[...] = both.T
    scores_two[...] = folded_dot(both, fold_two[...])


def pack(x):
    return jnp.concatenate([x[24 * k : 24 * k + 24] for k in range(8)], 1)


def unpack(x):
    return jnp.concatenate([x[:, HEADS * k : HEADS * (k + 1)] for k in range(8)], 0)


def stats_kernel(agg, cot, scores_two, dw_two, stats):
    heads = spread(1)
    score, grad = [[], []], [[], []]
    for b in range(NB):
        cot_f = cot[b * BLK : (b + 1) * BLK].astype(F32)
        for g in range(GR):
            rows = slice(b * AGG + g * BLK, b * AGG + (g + 1) * BLK)
            dw = head_sum(agg[rows].astype(F32) * cot_f, heads)
            dw_two[rows] = dw
            grad[g].append(dw)
            score[g].append(scores_two[rows])
    score = [jnp.concatenate(s, 0) for s in score]
    grad = [jnp.concatenate(s, 0) for s in grad]
    top = jnp.maximum(score[0], score[1])
    expo = [jnp.exp(s - top) for s in score]
    total = expo[0] + expo[1]
    log_total = top + jnp.log(total)
    inner = (expo[0] * grad[0] + expo[1] * grad[1]) / total
    both = jnp.concatenate([pack(log_total), pack(inner)], 0)
    for k in range(16):
        stats[k] = both


def backward_kernel(
    table, core, stats, agg_t, tok_t, cot, scores_two, dw_two, values, weights,
    w_key, w_key_two, fold_two,
    value_grad, score_grad, send, keep, sums,
):
    heads, heads2 = spread(1), spread(2)
    group = [table[c] for c in range(CH)]
    logs = stats[:, :24, :]
    top = jnp.max(logs, 0)
    expo = jnp.exp(logs - top[None])
    total = jnp.sum(expo, 0)
    inner = unpack(jnp.sum(expo * stats[:, 24:, :], 0) / total)
    log_total = unpack(top + jnp.log(total))
    grads_two = []
    for b in range(NB):
        rows = slice(b * BLK, (b + 1) * BLK)
        arows = slice(b * AGG, (b + 1) * AGG)
        trows = slice(b * TOK, (b + 1) * TOK)
        twice = lambda x: jnp.concatenate([x, x], 0)
        w_two = jnp.exp(scores_two[arows] - twice(log_total[rows]))
        s_two = w_two * (dw_two[arows] - twice(inner[rows]))
        grads_two.append(s_two)
        cot_f = cot[rows].astype(F32)
        agg_grad = expand(w_two, heads2) * twice(cot_f) + folded_back(s_two, fold_two[...])
        agg_grad = agg_grad.astype(BF16).astype(F32)
        first, second = agg_grad[:BLK], agg_grad[BLK:]
        chan = jnp.concatenate([jnp.where(group[c] == 0, first, second) for c in range(CH)], 0)
        weight = weights[trows]
        value_grad[trows] = (expand(weight, heads2) * chan).astype(BF16)
        dw = head_sum(chan * values[trows], heads)
        wdw = weight * dw
        part = [wdw[c * BLK : (c + 1) * BLK] for c in range(CH)]
        inner_one = [
            sum(jnp.where(group[c] == g, part[c], 0.0) for c in range(CH)) for g in range(GR)
        ]
        own = jnp.concatenate(
            [jnp.where(group[c] == 0, inner_one[0], inner_one[1]) for c in range(CH)], 0
        )
        score_grad[trows] = weight * (dw - own)
    for n in range(4):
        cols = slice(n * 256, (n + 1) * 256)
        out = nn(tok_t[...], value_grad[:, cols])
        for p in range(16):
            sums[p * SLAB : p * SLAB + 64, cols] = out[p * 64 : (p + 1) * 64]

    def outer(left, right):
        both = nn(left, jnp.concatenate(split2(right), 1))
        return both[:, :HEADS] + both[:, HEADS:]

    ones = outer(tok_t[...], score_grad[...])
    twos = outer(agg_t[...], jnp.concatenate(grads_two, 0))
    grads = jnp.concatenate([ones, twos, jnp.zeros((D, 128 - 2 * HEADS), F32)], 1).T
    lines = []
    for k, weight in enumerate((w_key, w_key_two)):
        high, low = split2(grads[k * HEADS : (k + 1) * HEADS])
        out = nn(jnp.concatenate([high, low], 0), weight[...])
        out = (out[:HEADS] + out[HEADS:]) * heads.astype(F32)
        lines.append(jnp.sum(out, 0, keepdims=True) * SCALE)
    quads = jnp.concatenate(
        [lines[0][:, :512], lines[0][:, 512:], lines[1][:, :512], lines[1][:, 512:]], 0
    )
    high = quads.astype(BF16).astype(F32)
    small = jnp.concatenate([high, quads - high], 0)
    turned = jnp.concatenate([grads[: 2 * HEADS, 64:], grads[: 2 * HEADS, :64]], 1)
    for p in range(16):
        source = turned if p % 2 else grads
        rows = slice(p * SLAB + 64, (p + 1) * SLAB)
        lanes = slice((p // 2) * 128, (p // 2 + 1) * 128)
        for k in range(4):
            sums[rows, k * 128 : (k + 1) * 128] = source[8 * k : 8 * k + 8, lanes]
        sums[rows, 512:] = small
    mine = core[0]
    for k in range(8):
        away = pl.multiple_of((2 * k + 1 - mine) * SLAB, 8)
        here = pl.multiple_of((2 * k + mine) * SLAB, 8)
        send[k] = sums[pl.ds(away, SLAB), :].astype(BF16)
        keep[k] = sums[pl.ds(here, SLAB), :]


def token_kernel(value_grad, score_grad, w_value, fold_one, out):
    grad = nt(value_grad[...], w_value[...]) + folded_back(score_grad[...], fold_one[...])
    out[...] = grad.astype(BF16).reshape(CH, BLK, D)


def rows_kernel(got, out):
    total = got[0].astype(F32)
    for k in range(1, 8):
        total = total + got[k].astype(F32)
    extra = total[64:]
    tall = [extra[:, k * 128 : k * 128 + 64] for k in range(4)]
    line = extra[:4, 512:] + extra[4:, 512:]
    extra = jnp.concatenate([t[:4] for t in tall] + [t[4:] for t in tall] + [line], 1)
    for c in range(16):
        out[c] = jnp.concatenate([total[4 * c : 4 * c + 4], extra], 0).astype(BF16)


def chans_kernel(got, rows, extra):
    total = got[0].astype(F32)
    for k in range(1, 16):
        total = total + got[k].astype(F32)
    for c in range(16):
        rows[c] = total[:4]
    extra[...] = total[4:]


def small_kernel(extra, query_one, query_two, grad_key, grad_key_two, line_one, line_two):
    x = extra[...]
    tall = [x[:, k * 64 : (k + 1) * 64] for k in range(8)]
    grads = jnp.concatenate(
        [jnp.concatenate([tall[k], tall[k + 4]], 0) for k in range(4)], 0
    )
    grads = jnp.concatenate([grads, jnp.zeros((32, 64), F32)], 0)
    turned = jnp.concatenate([grads, jnp.zeros((64, 64), F32)], 1).T[:64]
    heads3 = spread(3)
    for k, (query, out) in enumerate(((query_one, grad_key), (query_two, grad_key_two))):
        part = turned[:, k * HEADS : (k + 1) * HEADS]
        out[...] = nn(jnp.concatenate(split3(part), 1), heads3) * (query[...] * SCALE)
    line_one[:, :512] = x[0:1, 512:]
    line_one[:, 512:] = x[1:2, 512:]
    line_two[:, :512] = x[2:3, 512:]
    line_two[:, 512:] = x[3:4, 512:]


def shape(dims, dtype):
    return jax.ShapeDtypeStruct(dims, dtype)


SMEM = pl.BlockSpec(memory_space=pltpu.SMEM)


def whole(dims):
    return pl.BlockSpec(dims, lambda i: (0,) * len(dims))


def call(kernel, out_shape, flops, nbytes, **kw):
    return pl.pallas_call(
        kernel,
        out_shape=out_shape,
        compiler_params=pltpu.CompilerParams(vmem_limit_bytes=LIMIT),
        cost_estimate=pl.CostEstimate(flops=flops, bytes_accessed=nbytes, transcendentals=0),
        **kw,
    )


def shards(tokens, table, w_key, w_value, query_one, w_key_two, query_two, cotangent):
    query_one, query_two = query_one.reshape(1, D), query_two.reshape(1, D)
    tiled = jnp.broadcast_to(cotangent, (16, ROWS // 16, D)).reshape(ROWS, D)
    cot = lax.all_to_all(tiled, "chan", 0, 0, tiled=True)
    full = whole((D, D))
    by_rows = lambda n, w: pl.BlockSpec((n, w), lambda i: (i, 0))
    by_cols = lambda n: pl.BlockSpec((D, n), lambda i: (0, i))
    token_spec = pl.BlockSpec((CH, BLK, D), lambda i: (0, i, 0))
    values, weights, agg, agg_t, tok_t, scores_two, fold_one, fold_two = call(
        forward_kernel,
        (
            shape((NB * TOK, D), F32),
            shape((NB * TOK, HEADS), F32),
            shape((NB * AGG, D), BF16),
            shape((D, NB * AGG), BF16),
            shape((D, NB * TOK), BF16),
            shape((NB * AGG, HEADS), F32),
            shape((D, 3 * HEADS), BF16),
            shape((D, 3 * HEADS), BF16),
        ),
        4 * 10**9,
        16 * 10**6,
        grid=(NB,),
        in_specs=[SMEM, token_spec, full, full, full, whole((1, D)), whole((1, D))],
        out_specs=(
            by_rows(TOK, D),
            by_rows(TOK, HEADS),
            by_rows(AGG, D),
            by_cols(AGG),
            by_cols(TOK),
            by_rows(AGG, HEADS),
            whole((D, 3 * HEADS)),
            whole((D, 3 * HEADS)),
        ),
    )(table, tokens, w_value, w_key, w_key_two, query_one, query_two)
    dw_two, stats = call(
        stats_kernel,
        (shape((NB * AGG, HEADS), F32), shape((16, 48, 128), F32)),
        10**9,
        2 * 10**6,
    )(agg, cot, scores_two)
    stats = lax.all_to_all(stats, "chan", 0, 0, tiled=True)
    core = lax.rem(lax.axis_index("patch"), 2).astype(jnp.int32).reshape(1)
    vmem = pl.BlockSpec(memory_space=pltpu.VMEM)
    value_grad, score_grad, send, keep = call(
        backward_kernel,
        (
            shape((NB * TOK, D), BF16),
            shape((NB * TOK, HEADS), F32),
            shape((8, SLAB, D), BF16),
            shape((8, SLAB, D), F32),
        ),
        4 * 10**9,
        16 * 10**6,
        in_specs=[SMEM, SMEM] + [vmem] * 11,
        scratch_shapes=[pltpu.VMEM((16 * SLAB, D), F32)],
    )(
        table, core, stats, agg_t, tok_t, cot, scores_two, dw_two, values, weights,
        w_key, w_key_two, fold_two,
    )
    got = lax.ppermute(send, "patch", [(i, i ^ 1) for i in range(16)])
    pairs = (keep + got.astype(F32)).astype(BF16)
    same_core = [[i for i in range(16) if i % 2 == k] for k in range(2)]
    got = lax.all_to_all(pairs, "patch", 0, 0, tiled=True, axis_index_groups=same_core)
    token_grad = call(
        token_kernel,
        shape((CH, ROWS, D), BF16),
        2 * 10**9,
        6 * 10**6,
        grid=(NB,),
        in_specs=[by_rows(TOK, D), by_rows(TOK, HEADS), full, whole((D, 3 * HEADS))],
        out_specs=token_spec,
    )(value_grad, score_grad, w_value, fold_one)
    rows = call(rows_kernel, shape((16, 8, D), BF16), 10**6, 2 * 10**6)(got)
    rows = lax.all_to_all(rows, "chan", 0, 0, tiled=True)
    rows, extra = call(
        chans_kernel, (shape((16, 4, D), F32), shape((4, D), F32)), 10**6, 10**6
    )(rows)
    rows = lax.all_to_all(rows, "chan", 0, 0, tiled=True)
    grad_key, grad_key_two, line_one, line_two = call(
        small_kernel,
        (shape((64, D), F32), shape((64, D), F32), shape((1, D), F32), shape((1, D), F32)),
        10**8,
        10**6,
    )(extra, query_one, query_two)
    return (
        token_grad,
        grad_key,
        rows.reshape(64, D),
        grad_key_two,
        line_one.reshape(D),
        line_two.reshape(D),
    )


def solution(mesh):
    return jax.shard_map(
        shards,
        mesh=mesh,
        in_specs=(
            P("chan", "patch", None),
            P("chan"),
            P(),
            P(),
            P(),
            P(),
            P(),
            P("patch", "chan", None),
        ),
        out_specs=(
            P("chan", "patch", None),
            P("patch", None),
            P("patch", None),
            P("patch", None),
            P(),
            P(),
        ),
        check_vma=False,
    )
```

```python
import functools

import jax
import jax.numpy as jnp
from jax import lax
from jax.experimental import pallas as pl
from jax.experimental.pallas import tpu as pltpu
from jax.sharding import PartitionSpec as P

D = 1024
HEADS = 16
HD = 64
SHIFT = 6
SCALE = 0.125
CH = 4
GR = 2
ROWS = 192
BLK = 64
NB = ROWS // BLK
TOK = CH * BLK
AGG = GR * BLK
PAIRS = HEADS * HEADS
SLAB = 72
F32 = jnp.float32
BF16 = jnp.bfloat16
MIB = 2**20


def nn(a, b):
    return lax.dot_general(a, b, (((1,), (0,)), ((), ())), preferred_element_type=F32)


def nt(a, b):
    return lax.dot_general(a, b, (((1,), (1,)), ((), ())), preferred_element_type=F32)


def split2(x):
    high = x.astype(BF16)
    return high, (x - high.astype(F32)).astype(BF16)


def split3(x):
    high = x.astype(BF16)
    rest = x - high.astype(F32)
    middle = rest.astype(BF16)
    return high, middle, (rest - middle.astype(F32)).astype(BF16)


def spread(copies):
    row = lax.broadcasted_iota(jnp.int32, (copies * HEADS, D), 0) & (HEADS - 1)
    col = lax.broadcasted_iota(jnp.int32, (copies * HEADS, D), 1) >> SHIFT
    return jnp.where(row == col, 1.0, 0.0).astype(BF16)


def expand(x, heads2):
    return nn(jnp.concatenate(split2(x), 1), heads2)


def head_sum(x, heads):
    high, low = split2(x)
    return nt(high, heads) + nt(low, heads)


def fold(weight, query):
    parts = [p.astype(F32) for p in split3(query * SCALE)]
    row = lax.broadcasted_iota(jnp.int32, (HEADS, D), 0)
    col = lax.broadcasted_iota(jnp.int32, (HEADS, D), 1) >> SHIFT
    wide = [jnp.where(row == col, p, 0.0).astype(BF16) for p in parts]
    out = nt(weight, jnp.concatenate(wide, 0))
    total = out[:, :HEADS] + out[:, HEADS : 2 * HEADS] + out[:, 2 * HEADS :]
    return jnp.concatenate(split3(total), 1)


def folded_dot(x, folded):
    out = nn(x, folded)
    return out[:, :HEADS] + out[:, HEADS : 2 * HEADS] + out[:, 2 * HEADS :]


def folded_back(x, folded):
    high, low = split2(x)
    right = jnp.concatenate(
        [folded[:, :HEADS], folded[:, HEADS : 2 * HEADS], folded[:, :HEADS]], 1
    )
    return nt(jnp.concatenate([high, high, low], 1), right)


def forward_kernel(
    table, tok, w_value, w_key, w_key_two, query_one, query_two,
    values, weights, agg, agg_t, tok_t, scores_two, fold_one, fold_two,
):
    @pl.when(pl.program_id(0) == 0)
    def _():
        fold_one[...] = fold(w_key[...], query_one[...])
        fold_two[...] = fold(w_key_two[...], query_two[...])

    flat = tok[...].reshape(TOK, D)
    tok_t[...] = flat.T
    scores = folded_dot(flat, fold_one[...])
    vals = nn(flat, w_value[...])
    values[...] = vals
    group = [table[c] for c in range(CH)]
    score = [scores[c * BLK : (c + 1) * BLK] for c in range(CH)]
    top = [
        functools.reduce(
            jnp.maximum, [jnp.where(group[c] == g, score[c], -jnp.inf) for c in range(CH)]
        )
        for g in range(GR)
    ]
    expo = [jnp.exp(score[c] - jnp.where(group[c] == 0, top[0], top[1])) for c in range(CH)]
    total = [sum(jnp.where(group[c] == g, expo[c], 0.0) for c in range(CH)) for g in range(GR)]
    weight = jnp.concatenate(
        [expo[c] / jnp.where(group[c] == 0, total[0], total[1]) for c in range(CH)], 0
    )
    weights[...] = weight
    mixed = expand(weight, spread(2)) * vals
    part = [mixed[c * BLK : (c + 1) * BLK] for c in range(CH)]
    both = jnp.concatenate(
        [sum(jnp.where(group[c] == g, part[c], 0.0) for c in range(CH)) for g in range(GR)], 0
    ).astype(BF16)
    agg[...] = both
    agg_t[...] = both.T
    scores_two[...] = folded_dot(both, fold_two[...])


def pack(x):
    return jnp.concatenate([x[24 * k : 24 * k + 24] for k in range(8)], 1)


def unpack(x):
    return jnp.concatenate([x[:, HEADS * k : HEADS * (k + 1)] for k in range(8)], 0)


def tile_kernel(cot, out):
    for k in range(16):
        out[k] = cot[0]


def stats_kernel(agg, got, scores_two, dw_two, stats, cot, rows_f):
    heads = spread(1)
    for k in range(16):
        rows_f[12 * k : 12 * k + 12] = got[k].astype(F32)
    cot[...] = rows_f[...].astype(BF16)
    score, grad = [[], []], [[], []]
    for b in range(NB):
        cot_f = rows_f[b * BLK : (b + 1) * BLK]
        for g in range(GR):
            rows = slice(b * AGG + g * BLK, b * AGG + (g + 1) * BLK)
            dw = head_sum(agg[rows].astype(F32) * cot_f, heads)
            dw_two[rows] = dw
            grad[g].append(dw)
            score[g].append(scores_two[rows])
    score = [jnp.concatenate(s, 0) for s in score]
    grad = [jnp.concatenate(s, 0) for s in grad]
    top = jnp.maximum(score[0], score[1])
    expo = [jnp.exp(s - top) for s in score]
    total = expo[0] + expo[1]
    log_total = top + jnp.log(total)
    inner = (expo[0] * grad[0] + expo[1] * grad[1]) / total
    both = jnp.concatenate([pack(log_total), pack(inner)], 0)
    for k in range(16):
        stats[k] = both


def pre_kernel(values, cot, fold_two, direct, cross):
    heads = spread(1)
    row = lax.broadcasted_iota(jnp.int32, (HEADS, PAIRS), 0)
    col = lax.broadcasted_iota(jnp.int32, (HEADS, PAIRS), 1)
    copies = jnp.where(row == (col & (HEADS - 1)), 1.0, 0.0).astype(BF16)
    own = (lax.broadcasted_iota(jnp.int32, (D, PAIRS), 0) >> SHIFT) == (
        lax.broadcasted_iota(jnp.int32, (D, PAIRS), 1) >> 4
    )
    wide = [
        jnp.where(own, nn(fold_two[:, k * HEADS : (k + 1) * HEADS], copies), 0.0).astype(BF16)
        for k in range(2)
    ]
    for b in range(NB):
        trows = slice(b * TOK, (b + 1) * TOK)
        cot_f = cot[b * BLK : (b + 1) * BLK].astype(F32)
        vals = values[trows]
        direct[trows] = head_sum(jnp.concatenate([cot_f] * CH, 0) * vals, heads)
        high, low = split2(vals)
        cross[trows] = nn(high, wide[0]) + nn(high, wide[1]) + nn(low, wide[0])


def back_kernel(
    table, core, stats, cot_h, scores_h, dw_h, weights_h, fold_h, direct_h, cross_h, tok_h, agg_h,
    key_h, key_two_h,
    value_grad, score_grad_h, send_h, keep_h,
    cot, scores_two, dw_two, weights, fold_two, direct, cross, tok_t, agg_t, w_key, w_key_two,
    grad, sums, send, keep, score_grad, sems,
):
    sources = (
        cot_h, scores_h, dw_h, weights_h, fold_h, tok_h, direct_h, cross_h, agg_h, key_h, key_two_h,
    )
    targets = (
        cot, scores_two, dw_two, weights, fold_two, tok_t, direct, cross, agg_t, w_key, w_key_two,
    )
    copies = [
        pltpu.make_async_copy(x, y, sems.at[k]) for k, (x, y) in enumerate(zip(sources, targets))
    ]
    for c in copies[:5]:
        c.start()
    heads, heads2 = spread(1), spread(2)
    group = [table[c] for c in range(CH)]

    def by_channel(x):
        return jnp.concatenate(
            [jnp.where(group[c] == 0, x[:BLK], x[BLK:]) for c in range(CH)], 0
        )

    logs = stats[:, :24, :]
    top = jnp.max(logs, 0)
    expo = jnp.exp(logs - top[None])
    total = jnp.sum(expo, 0)
    inner = unpack(jnp.sum(expo * stats[:, 24:, :], 0) / total)
    log_total = unpack(top + jnp.log(total))
    for c in copies[:5]:
        c.wait()
    for c in copies[5:]:
        c.start()
    w_two, s_two = [], []
    for b in range(NB):
        rows = slice(b * BLK, (b + 1) * BLK)
        arows = slice(b * AGG, (b + 1) * AGG)
        trows = slice(b * TOK, (b + 1) * TOK)
        twice = lambda x: jnp.concatenate([x, x], 0)
        w_now = jnp.exp(scores_two[arows] - twice(log_total[rows]))
        s_now = w_now * (dw_two[arows] - twice(inner[rows]))
        w_two.append(w_now)
        s_two.append(s_now)
        cot_f = cot[rows].astype(F32)
        agg_grad = expand(w_now, heads2) * twice(cot_f) + folded_back(s_now, fold_two[...])
        grad[trows] = (expand(weights[trows], heads2) * by_channel(agg_grad)).astype(BF16)
    copies[5].wait()
    for n in range(4):
        cols = slice(n * 256, (n + 1) * 256)
        out = nn(tok_t[...], grad[:, cols])
        for p in range(16):
            sums[p * SLAB : p * SLAB + 64, cols] = out[p * 64 : (p + 1) * 64]
    row = lax.broadcasted_iota(jnp.int32, (2 * HEADS, PAIRS), 0) & (HEADS - 1)
    col = lax.broadcasted_iota(jnp.int32, (2 * HEADS, PAIRS), 1)
    tiled = jnp.where(row == (col & (HEADS - 1)), 1.0, 0.0).astype(BF16)
    gather = jnp.where(row == (col >> 4), 1.0, 0.0).astype(BF16)[:HEADS]
    copies[6].wait()
    copies[7].wait()
    for b in range(NB):
        trows = slice(b * TOK, (b + 1) * TOK)
        score = by_channel(s_two[b])
        product = nn(jnp.concatenate(split2(score), 1), tiled) * cross[trows]
        high, low = split2(product)
        dw = by_channel(w_two[b]) * direct[trows] + nt(high, gather) + nt(low, gather)
        weight = weights[trows]
        wdw = weight * dw
        part = [wdw[c * BLK : (c + 1) * BLK] for c in range(CH)]
        own = jnp.concatenate(
            [sum(jnp.where(group[c] == g, part[c], 0.0) for c in range(CH)) for g in range(GR)], 0
        )
        score_grad[trows] = weight * (dw - by_channel(own))

    def outer(left, right):
        both = nn(left, jnp.concatenate(split2(right), 1))
        return both[:, :HEADS] + both[:, HEADS:]

    started = [
        pltpu.make_async_copy(grad, value_grad, sems.at[11]),
        pltpu.make_async_copy(score_grad, score_grad_h, sems.at[14]),
    ]
    for c in started:
        c.start()
    ones = outer(tok_t[...], score_grad[...])
    copies[8].wait()
    twos = outer(agg_t[...], jnp.concatenate(s_two, 0))
    grads = jnp.concatenate([ones, twos, jnp.zeros((D, 128 - 2 * HEADS), F32)], 1).T[: 2 * HEADS]
    lines = []
    copies[9].wait()
    copies[10].wait()
    for k, weight in enumerate((w_key, w_key_two)):
        high, low = split2(grads[k * HEADS : (k + 1) * HEADS])
        out = nn(jnp.concatenate([high, low], 0), weight[...])
        out = (out[:HEADS] + out[HEADS:]) * heads.astype(F32)
        lines.append(jnp.sum(out, 0, keepdims=True) * SCALE)
    quarters = jnp.concatenate(
        [line[:, k * 256 : (k + 1) * 256] for line in lines for k in range(4)], 0
    )
    left = (lax.broadcasted_iota(jnp.int32, (8, D), 1) & 64) == 0
    pairs = []
    for odd in range(2):
        for k in range(2):
            one, two = grads[16 * k : 16 * k + 8], grads[16 * k + 8 : 16 * k + 16]
            if odd:
                one = jnp.concatenate([one[:, 64:], one[:, :64]], 1)
            else:
                two = jnp.concatenate([two[:, D - 64 :], two[:, : D - 64]], 1)
            pairs.append(jnp.where(left, one, two))
    for p in range(16):
        rows = slice(p * SLAB + 64, (p + 1) * SLAB)
        lanes = slice((p // 2) * 128, (p // 2 + 1) * 128)
        for half in (0, 512):
            for k in range(2):
                spot = slice(half + k * 128, half + (k + 1) * 128)
                sums[rows, spot] = pairs[2 * (p % 2) + k][:, lanes]
            sums[rows, half + 256 : half + 512] = quarters
    mine = core[0]
    for which, (held, target) in enumerate(((send, send_h), (keep, keep_h))):
        side = mine if which else 1 - mine
        for k in range(8):
            slab = sums[pl.ds(pl.multiple_of((2 * k + side) * SLAB, 8), SLAB), :]
            for half in range(2):
                held[8 * half + k] = slab[:, half * 512 : (half + 1) * 512].astype(held.dtype)
        started.append(pltpu.make_async_copy(held, target, sems.at[12 + which]))
        started[-1].start()
    for c in started:
        c.wait()


def pair_kernel(keep, got, out):
    out[...] = (keep[...].astype(F32) + got[...].astype(F32)).astype(BF16)


def token_kernel(value_grad, score_grad, w_value, fold_one, out):
    grad = nt(value_grad[...], w_value[...]) + folded_back(score_grad[...], fold_one[...])
    out[...] = grad.astype(BF16).reshape(CH, BLK, D)


def rows_kernel(got, out):
    total = got[0].astype(F32)
    for k in range(1, 16):
        total = total + got[k].astype(F32)
    total = total.astype(BF16)
    for z in range(8):
        out[z] = jnp.concatenate([total[8 * z : 8 * z + 8], total[64:]], 1)


def chans_kernel(got, rows, extra):
    total = got[0].astype(F32)
    for k in range(1, 8):
        total = total + got[k].astype(F32)
    own = total[:, :512].astype(BF16)
    for c in range(16):
        rows[c] = own
    extra[...] = total[:, 512:]


def last_kernel(got, out):
    for r in range(8):
        for half in range(2):
            out[8 * r : 8 * r + 8, half * 512 : (half + 1) * 512] = got[2 * r + half].astype(F32)


def small_kernel(extra, query_one, query_two, grad_key, grad_key_two, line_one, line_two):
    x = extra[...]
    grads = jnp.concatenate([x[:, k * 64 : (k + 1) * 64] for k in range(4)], 0)
    grads = jnp.concatenate([grads, jnp.zeros((96, 64), F32)], 0)
    turned = jnp.concatenate([grads, jnp.zeros((128, 64), F32)], 1).T[:64]
    heads3 = spread(3)
    for k, (query, out) in enumerate(((query_one, grad_key), (query_two, grad_key_two))):
        part = turned[:, k * HEADS : (k + 1) * HEADS]
        out[...] = nn(jnp.concatenate(split3(part), 1), heads3) * (query[...] * SCALE)
    for k in range(4):
        cols = slice(k * 256, (k + 1) * 256)
        line_one[:, cols] = x[k : k + 1, 256:]
        line_two[:, cols] = x[4 + k : 5 + k, 256:]


def shape(dims, dtype):
    return jax.ShapeDtypeStruct(dims, dtype)


SMEM = pl.BlockSpec(memory_space=pltpu.SMEM)


def whole(dims):
    return pl.BlockSpec(dims, lambda i: (0,) * len(dims))


def call(kernel, out_shape, flops, nbytes, limit=60, **kw):
    return pl.pallas_call(
        kernel,
        out_shape=out_shape,
        compiler_params=pltpu.CompilerParams(vmem_limit_bytes=limit * MIB),
        cost_estimate=pl.CostEstimate(flops=flops, bytes_accessed=nbytes, transcendentals=0),
        **kw,
    )


def shards(tokens, table, w_key, w_value, query_one, w_key_two, query_two, cotangent):
    query_one, query_two = query_one.reshape(1, D), query_two.reshape(1, D)
    tiled = call(tile_kernel, shape((16, ROWS // 16, D), BF16), 10**4, 10**6, 4)(cotangent)
    cot = lax.all_to_all(tiled, "chan", 0, 0, tiled=True)
    full = whole((D, D))
    by_rows = lambda n, w: pl.BlockSpec((n, w), lambda i: (i, 0))
    by_cols = lambda n: pl.BlockSpec((D, n), lambda i: (0, i))
    token_spec = pl.BlockSpec((CH, BLK, D), lambda i: (0, i, 0))
    values, weights, agg, agg_t, tok_t, scores_two, fold_one, fold_two = call(
        forward_kernel,
        (
            shape((NB * TOK, D), F32),
            shape((NB * TOK, HEADS), F32),
            shape((NB * AGG, D), BF16),
            shape((D, NB * AGG), BF16),
            shape((D, NB * TOK), BF16),
            shape((NB * AGG, HEADS), F32),
            shape((D, 3 * HEADS), BF16),
            shape((D, 3 * HEADS), BF16),
        ),
        4 * 10**9,
        16 * 10**6,
        grid=(NB,),
        in_specs=[SMEM, token_spec, full, full, full, whole((1, D)), whole((1, D))],
        out_specs=(
            by_rows(TOK, D),
            by_rows(TOK, HEADS),
            by_rows(AGG, D),
            by_cols(AGG),
            by_cols(TOK),
            by_rows(AGG, HEADS),
            whole((D, 3 * HEADS)),
            whole((D, 3 * HEADS)),
        ),
    )(table, tokens, w_value, w_key, w_key_two, query_one, query_two)
    dw_two, stats, cot = call(
        stats_kernel,
        (shape((NB * AGG, HEADS), F32), shape((16, 48, 128), F32), shape((ROWS, D), BF16)),
        10**9,
        2 * 10**6,
        scratch_shapes=[pltpu.VMEM((ROWS, D), F32)],
    )(agg, cot, scores_two)
    stats, fold_now = lax.optimization_barrier((stats, fold_two))
    stats = lax.all_to_all(stats, "chan", 0, 0, tiled=True)
    core = lax.rem(lax.axis_index("patch"), 2).astype(jnp.int32).reshape(1)
    direct, cross = call(
        pre_kernel,
        (shape((NB * TOK, HEADS), F32), shape((NB * TOK, PAIRS), F32)),
        10**9,
        5 * 10**6,
    )(values, cot, fold_now)
    vmem = pl.BlockSpec(memory_space=pltpu.VMEM)
    hbm = pl.BlockSpec(memory_space=pltpu.HBM)
    fetched = (
        cot, scores_two, dw_two, weights, fold_two, direct, cross, tok_t, agg_t, w_key, w_key_two,
    )
    value_grad, score_grad, send, keep = call(
        back_kernel,
        (
            shape((NB * TOK, D), BF16),
            shape((NB * TOK, HEADS), F32),
            shape((16, SLAB, 512), BF16),
            shape((16, SLAB, 512), BF16),
        ),
        4 * 10**9,
        16 * 10**6,
        in_specs=[SMEM, SMEM, vmem] + [hbm] * len(fetched),
        out_specs=(hbm, hbm, hbm, hbm),
        scratch_shapes=[pltpu.VMEM(x.shape, x.dtype) for x in fetched]
        + [
            pltpu.VMEM((NB * TOK, D), BF16),
            pltpu.VMEM((16 * SLAB, D), F32),
            pltpu.VMEM((16, SLAB, 512), BF16),
            pltpu.VMEM((16, SLAB, 512), BF16),
            pltpu.VMEM((NB * TOK, HEADS), F32),
            pltpu.SemaphoreType.DMA((15,)),
        ],
    )(table, core, stats, *fetched)
    got = lax.ppermute(send, "patch", [(i, i ^ 1) for i in range(16)])
    slabs = pl.BlockSpec((4, SLAB, 512), lambda i: (i, 0, 0))
    pairs = call(
        pair_kernel,
        shape((16, SLAB, 512), BF16),
        10**6,
        5 * 10**6,
        12,
        grid=(4,),
        in_specs=[slabs, slabs],
        out_specs=slabs,
    )(keep, got)
    planes = [
        [(2 * z + h) * 16 + 2 * k + core_bit for h in range(2) for k in range(8)]
        for z in range(8)
        for core_bit in range(2)
    ]
    got = lax.all_to_all(
        pairs, ("chan", "patch"), 0, 0, tiled=True, axis_index_groups=planes
    )
    token_grad = call(
        token_kernel,
        shape((CH, ROWS, D), BF16),
        2 * 10**9,
        6 * 10**6,
        24,
        grid=(NB,),
        in_specs=[by_rows(TOK, D), by_rows(TOK, HEADS), full, whole((D, 3 * HEADS))],
        out_specs=token_spec,
    )(value_grad, score_grad, w_value, fold_one)
    rows = call(rows_kernel, shape((8, 8, D), BF16), 10**6, 2 * 10**6, 8)(got)
    same_half = [[2 * z + h for z in range(8)] for h in range(2)]
    rows = lax.all_to_all(rows, "chan", 0, 0, tiled=True, axis_index_groups=same_half)
    rows, extra = call(
        chans_kernel, (shape((16, 8, 512), BF16), shape((8, 512), F32)), 10**6, 10**6, 8
    )(rows)
    rows = lax.all_to_all(rows, "chan", 0, 0, tiled=True)
    grad_value = call(last_kernel, shape((64, D), F32), 10**6, 10**6, 8)(rows)
    grad_key, grad_key_two, line_one, line_two = call(
        small_kernel,
        (shape((64, D), F32), shape((64, D), F32), shape((1, D), F32), shape((1, D), F32)),
        10**8,
        10**6,
        8,
    )(extra, query_one, query_two)
    return (
        token_grad,
        grad_key,
        grad_value,
        grad_key_two,
        line_one.reshape(D),
        line_two.reshape(D),
    )


def solution(mesh):
    return jax.shard_map(
        shards,
        mesh=mesh,
        in_specs=(
            P("chan", "patch", None),
            P("chan"),
            P(),
            P(),
            P(),
            P(),
            P(),
            P("patch", "chan", None),
        ),
        out_specs=(
            P("chan", "patch", None),
            P("patch", None),
            P("patch", None),
            P("patch", None),
            P(),
            P(),
        ),
        check_vma=False,
    )
```

```python
import functools

import jax
import jax.numpy as jnp
from jax import lax
from jax.experimental import pallas as pl
from jax.experimental.pallas import tpu as pltpu
from jax.sharding import PartitionSpec as P

D = 1024
HEADS = 16
HD = 64
SHIFT = 6
SCALE = 0.125
CH = 4
GR = 2
ROWS = 192
BLK = 64
NB = ROWS // BLK
TOK = CH * BLK
AGG = GR * BLK
PAIRS = HEADS * HEADS
SLAB = 72
F32 = jnp.float32
BF16 = jnp.bfloat16
MIB = 2**20


def nn(a, b):
    return lax.dot_general(a, b, (((1,), (0,)), ((), ())), preferred_element_type=F32)


def nt(a, b):
    return lax.dot_general(a, b, (((1,), (1,)), ((), ())), preferred_element_type=F32)


def split2(x):
    high = x.astype(BF16)
    return high, (x - high.astype(F32)).astype(BF16)


def split3(x):
    high = x.astype(BF16)
    rest = x - high.astype(F32)
    middle = rest.astype(BF16)
    return high, middle, (rest - middle.astype(F32)).astype(BF16)


def spread(copies):
    row = lax.broadcasted_iota(jnp.int32, (copies * HEADS, D), 0) & (HEADS - 1)
    col = lax.broadcasted_iota(jnp.int32, (copies * HEADS, D), 1) >> SHIFT
    return jnp.where(row == col, 1.0, 0.0).astype(BF16)


def expand(x, heads2):
    return nn(jnp.concatenate(split2(x), 1), heads2)


def head_sum(x, heads):
    high, low = split2(x)
    return nt(high, heads) + nt(low, heads)


def fold(weight, query):
    parts = [p.astype(F32) for p in split3(query * SCALE)]
    row = lax.broadcasted_iota(jnp.int32, (HEADS, D), 0)
    col = lax.broadcasted_iota(jnp.int32, (HEADS, D), 1) >> SHIFT
    wide = [jnp.where(row == col, p, 0.0).astype(BF16) for p in parts]
    out = nt(weight, jnp.concatenate(wide, 0))
    total = out[:, :HEADS] + out[:, HEADS : 2 * HEADS] + out[:, 2 * HEADS :]
    return jnp.concatenate(split3(total), 1)


def folded_dot(x, folded):
    out = nn(x, folded)
    return out[:, :HEADS] + out[:, HEADS : 2 * HEADS] + out[:, 2 * HEADS :]


def folded_back(x, folded):
    high, low = split2(x)
    right = jnp.concatenate(
        [folded[:, :HEADS], folded[:, HEADS : 2 * HEADS], folded[:, :HEADS]], 1
    )
    return nt(jnp.concatenate([high, high, low], 1), right)


def forward_kernel(
    table, tok, w_value, w_key, w_key_two, query_one, query_two,
    values, weights, agg, agg_t, tok_t, scores_two, fold_one, fold_two, cross,
    wide,
):
    @pl.when(pl.program_id(0) == 0)
    def _():
        fold_one[...] = fold(w_key[...], query_one[...])
        fold_two[...] = fold(w_key_two[...], query_two[...])
        row = lax.broadcasted_iota(jnp.int32, (HEADS, PAIRS), 0)
        col = lax.broadcasted_iota(jnp.int32, (HEADS, PAIRS), 1)
        copies = jnp.where(row == (col & (HEADS - 1)), 1.0, 0.0).astype(BF16)
        own = (lax.broadcasted_iota(jnp.int32, (D, PAIRS), 0) >> SHIFT) == (
            lax.broadcasted_iota(jnp.int32, (D, PAIRS), 1) >> 4
        )
        for k in range(2):
            spot = nn(fold_two[:, k * HEADS : (k + 1) * HEADS], copies)
            wide[k] = jnp.where(own, spot, 0.0).astype(BF16)

    flat = tok[...].reshape(TOK, D)
    tok_t[...] = flat.T
    scores = folded_dot(flat, fold_one[...])
    vals = nn(flat, w_value[...])
    values[...] = vals
    high, low = split2(vals)
    cross[...] = nn(high, wide[0]) + nn(high, wide[1]) + nn(low, wide[0])
    group = [table[c] for c in range(CH)]
    score = [scores[c * BLK : (c + 1) * BLK] for c in range(CH)]
    top = [
        functools.reduce(
            jnp.maximum, [jnp.where(group[c] == g, score[c], -jnp.inf) for c in range(CH)]
        )
        for g in range(GR)
    ]
    expo = [jnp.exp(score[c] - jnp.where(group[c] == 0, top[0], top[1])) for c in range(CH)]
    total = [sum(jnp.where(group[c] == g, expo[c], 0.0) for c in range(CH)) for g in range(GR)]
    weight = jnp.concatenate(
        [expo[c] / jnp.where(group[c] == 0, total[0], total[1]) for c in range(CH)], 0
    )
    weights[...] = weight
    mixed = expand(weight, spread(2)) * vals
    part = [mixed[c * BLK : (c + 1) * BLK] for c in range(CH)]
    both = jnp.concatenate(
        [sum(jnp.where(group[c] == g, part[c], 0.0) for c in range(CH)) for g in range(GR)], 0
    ).astype(BF16)
    agg[...] = both
    agg_t[...] = both.T
    scores_two[...] = folded_dot(both, fold_two[...])


def pack(x):
    return jnp.concatenate([x[24 * k : 24 * k + 24] for k in range(8)], 1)


def unpack(x):
    return jnp.concatenate([x[:, HEADS * k : HEADS * (k + 1)] for k in range(8)], 0)


def tile_kernel(cot, out):
    for k in range(16):
        out[k] = cot[0]


def stats_kernel(agg, cot, scores_two, pair_two, stats):
    heads = spread(1)
    score, grad = [[], []], [[], []]
    for b in range(NB):
        cot_f = cot[b * BLK : (b + 1) * BLK].astype(F32)
        for g in range(GR):
            rows = slice(b * AGG + g * BLK, b * AGG + (g + 1) * BLK)
            dw = head_sum(agg[rows].astype(F32) * cot_f, heads)
            grad[g].append(dw)
            score[g].append(scores_two[rows])
            pair_two[rows] = jnp.concatenate([score[g][-1], dw], 1)
    score = [jnp.concatenate(s, 0) for s in score]
    grad = [jnp.concatenate(s, 0) for s in grad]
    top = jnp.maximum(score[0], score[1])
    expo = [jnp.exp(s - top) for s in score]
    total = expo[0] + expo[1]
    log_total = top + jnp.log(total)
    inner = (expo[0] * grad[0] + expo[1] * grad[1]) / total
    both = jnp.concatenate([pack(log_total), pack(inner)], 0)
    for k in range(16):
        stats[k] = both


def pre_kernel(values, cot, weights, direct):
    heads = spread(1)
    for b in range(NB):
        trows = slice(b * TOK, (b + 1) * TOK)
        cot_f = cot[b * BLK : (b + 1) * BLK].astype(F32)
        direct[trows] = jnp.concatenate(
            [weights[trows], head_sum(jnp.concatenate([cot_f] * CH, 0) * values[trows], heads)], 1
        )


def total_kernel(stats, out):
    logs = stats[:, :24, :]
    top = jnp.max(logs, 0)
    expo = jnp.exp(logs - top[None])
    total = jnp.sum(expo, 0)
    out[:24] = top + jnp.log(total)
    out[24:] = jnp.sum(expo * stats[:, 24:, :], 0) / total


def back_kernel(
    table, core, totals, cot_h, pair_h, weights_h, fold_h, tok_h, cross_h, agg_h, key_h, key_two_h,
    value_grad, score_grad_h, send_h, extra,
    cot, pair_two, weights, fold_two, tok_t, cross, agg_t, w_key, w_key_two,
    grad, send, score_grad, sems,
):
    sources = (cot_h, pair_h, weights_h, fold_h, tok_h, cross_h, agg_h, key_h, key_two_h)
    targets = (cot, pair_two, weights, fold_two, tok_t, cross, agg_t, w_key, w_key_two)
    copies = [
        pltpu.make_async_copy(x, y, sems.at[k]) for k, (x, y) in enumerate(zip(sources, targets))
    ]
    for c in copies[:5]:
        c.start()
    heads, heads2 = spread(1), spread(2)
    group = [table[c] for c in range(CH)]

    def by_channel(x):
        return jnp.concatenate(
            [jnp.where(group[c] == 0, x[:BLK], x[BLK:]) for c in range(CH)], 0
        )

    log_total, inner = unpack(totals[:24]), unpack(totals[24:])
    for c in copies[:4]:
        c.wait()
    for c in copies[5:]:
        c.start()
    w_two, s_two = [], []
    for b in range(NB):
        rows = slice(b * BLK, (b + 1) * BLK)
        arows = slice(b * AGG, (b + 1) * AGG)
        trows = slice(b * TOK, (b + 1) * TOK)
        twice = lambda x: jnp.concatenate([x, x], 0)
        w_now = jnp.exp(pair_two[arows, :HEADS] - twice(log_total[rows]))
        s_now = w_now * (pair_two[arows, HEADS:] - twice(inner[rows]))
        w_two.append(w_now)
        s_two.append(s_now)
        cot_f = cot[rows].astype(F32)
        agg_grad = expand(w_now, heads2) * twice(cot_f) + folded_back(s_now, fold_two[...])
        weight = weights[trows, :HEADS]
        grad[trows] = (expand(weight, heads2) * by_channel(agg_grad)).astype(BF16)
    copies[4].wait()
    copies[5].wait()
    row = lax.broadcasted_iota(jnp.int32, (2 * HEADS, PAIRS), 0) & (HEADS - 1)
    col = lax.broadcasted_iota(jnp.int32, (2 * HEADS, PAIRS), 1)
    tiled = jnp.where(row == (col & (HEADS - 1)), 1.0, 0.0).astype(BF16)
    gather = jnp.where(row == (col >> 4), 1.0, 0.0).astype(BF16)[:HEADS]
    for b in range(NB):
        trows = slice(b * TOK, (b + 1) * TOK)
        score = by_channel(s_two[b])
        product = nn(jnp.concatenate(split2(score), 1), tiled) * cross[trows]
        high, low = split2(product)
        direct = weights[trows, HEADS:]
        dw = by_channel(w_two[b]) * direct + nt(high, gather) + nt(low, gather)
        weight = weights[trows, :HEADS]
        wdw = weight * dw
        part = [wdw[c * BLK : (c + 1) * BLK] for c in range(CH)]
        own = jnp.concatenate(
            [sum(jnp.where(group[c] == g, part[c], 0.0) for c in range(CH)) for g in range(GR)], 0
        )
        score_grad[trows] = weight * (dw - by_channel(own))

    def outer(left, right):
        both = nn(left, jnp.concatenate(split2(right), 1))
        return both[:, :HEADS] + both[:, HEADS:]

    ones = outer(tok_t[...], score_grad[...])
    copies[6].wait()
    twos = outer(agg_t[...], jnp.concatenate(s_two, 0))
    grads = jnp.concatenate([ones, twos, jnp.zeros((D, 128 - 2 * HEADS), F32)], 1).T[: 2 * HEADS]
    copies[7].wait()
    copies[8].wait()
    started = [
        pltpu.make_async_copy(grad, value_grad, sems.at[9]),
        pltpu.make_async_copy(score_grad, score_grad_h, sems.at[10]),
    ]
    for c in started:
        c.start()
    lines = []
    for k, weight in enumerate((w_key, w_key_two)):
        high, low = split2(grads[k * HEADS : (k + 1) * HEADS])
        out = nn(jnp.concatenate([high, low], 0), weight[...])
        out = (out[:HEADS] + out[HEADS:]) * heads.astype(F32)
        lines.append(jnp.sum(out, 0, keepdims=True) * SCALE)
    quarters = jnp.concatenate(
        [line[:, k * 256 : (k + 1) * 256] for line in lines for k in range(4)], 0
    )
    left = (lax.broadcasted_iota(jnp.int32, (8, D), 1) & 64) == 0
    even, odd = [], []
    for k in range(2):
        one, two = grads[16 * k : 16 * k + 8], grads[16 * k + 8 : 16 * k + 16]
        even.append(jnp.where(left, one, jnp.concatenate([two[:, D - 64 :], two[:, : D - 64]], 1)))
        odd.append(jnp.where(left, jnp.concatenate([one[:, 64:], one[:, :64]], 1), two))
    mine = core[0]
    here = [jnp.where(mine == 0, x, y) for x, y in zip(even, odd)]
    away = [jnp.where(mine == 0, y, x) for x, y in zip(even, odd)]

    def small(pair, k):
        lanes = slice(k * 128, (k + 1) * 128)
        return jnp.concatenate([pair[0][:, lanes], pair[1][:, lanes], quarters], 1)

    for k in range(0, 8, 4):
        out = nn(peer_rows(tok_t, k, 1 - mine), grad[...])
        for i in range(4):
            extra[k + i] = small(here, k + i)
            other = small(away, k + i)
            for half in range(2):
                part = out[64 * i : 64 * (i + 1), half * 512 : (half + 1) * 512]
                send[8 * half + k + i] = jnp.concatenate([part, other], 0).astype(BF16)
    started.append(pltpu.make_async_copy(send, send_h, sems.at[11]))
    started[-1].start()
    for c in started:
        c.wait()


def peer_rows(tok_t, k, side):
    return jnp.concatenate(
        [tok_t[pl.ds(pl.multiple_of((2 * (k + i) + side) * 64, 64), 64), :] for i in range(4)], 0
    )


def keep_kernel(core, tok_t, value_grad, extra, keep):
    mine = core[0]
    for k in range(0, 8, 4):
        out = nn(peer_rows(tok_t, k, mine), value_grad[...])
        for i in range(4):
            for half in range(2):
                part = out[64 * i : 64 * (i + 1), half * 512 : (half + 1) * 512]
                keep[8 * half + k + i] = jnp.concatenate([part, extra[k + i]], 0)


def pair_kernel(keep, got, out):
    out[...] = (keep[...] + got[...].astype(F32)).astype(BF16)


def token_kernel(value_grad, score_grad, w_value, fold_one, out):
    grad = nt(value_grad[...], w_value[...]) + folded_back(score_grad[...], fold_one[...])
    out[...] = grad.astype(BF16).reshape(CH, BLK, D)


def rows_kernel(got, out):
    total = got[0].astype(F32)
    for k in range(1, 16):
        total = total + got[k].astype(F32)
    total = total.astype(BF16)
    for z in range(8):
        out[z] = jnp.concatenate([total[8 * z : 8 * z + 8], total[64:]], 1)


def chans_kernel(got, rows, extra):
    total = got[0].astype(F32)
    for k in range(1, 8):
        total = total + got[k].astype(F32)
    own = total[:, :512].astype(BF16)
    for c in range(16):
        rows[c] = own
    extra[...] = total[:, 512:]


def last_kernel(got, out):
    for r in range(8):
        for half in range(2):
            out[8 * r : 8 * r + 8, half * 512 : (half + 1) * 512] = got[2 * r + half].astype(F32)


def small_kernel(extra, query_one, query_two, grad_key, grad_key_two, line_one, line_two):
    x = extra[...]
    grads = jnp.concatenate([x[:, k * 64 : (k + 1) * 64] for k in range(4)], 0)
    grads = jnp.concatenate([grads, jnp.zeros((96, 64), F32)], 0)
    turned = jnp.concatenate([grads, jnp.zeros((128, 64), F32)], 1).T[:64]
    heads3 = spread(3)
    for k, (query, out) in enumerate(((query_one, grad_key), (query_two, grad_key_two))):
        part = turned[:, k * HEADS : (k + 1) * HEADS]
        out[...] = nn(jnp.concatenate(split3(part), 1), heads3) * (query[...] * SCALE)
    for k in range(4):
        cols = slice(k * 256, (k + 1) * 256)
        line_one[:, cols] = x[k : k + 1, 256:]
        line_two[:, cols] = x[4 + k : 5 + k, 256:]


def shape(dims, dtype):
    return jax.ShapeDtypeStruct(dims, dtype)


SMEM = pl.BlockSpec(memory_space=pltpu.SMEM)


def whole(dims):
    return pl.BlockSpec(dims, lambda i: (0,) * len(dims))


def call(kernel, out_shape, flops, nbytes, limit=60, **kw):
    return pl.pallas_call(
        kernel,
        out_shape=out_shape,
        compiler_params=pltpu.CompilerParams(vmem_limit_bytes=limit * MIB),
        cost_estimate=pl.CostEstimate(flops=flops, bytes_accessed=nbytes, transcendentals=0),
        **kw,
    )


def shards(tokens, table, w_key, w_value, query_one, w_key_two, query_two, cotangent):
    query_one, query_two = query_one.reshape(1, D), query_two.reshape(1, D)
    vmem = pl.BlockSpec(memory_space=pltpu.VMEM)
    hbm = pl.BlockSpec(memory_space=pltpu.HBM)
    tiled = call(
        tile_kernel,
        shape((16, ROWS // 16, D), BF16),
        10**4,
        10**6,
    )(cotangent)
    cot = lax.all_to_all(tiled, "chan", 0, 0, tiled=True).reshape(ROWS, D)
    full = whole((D, D))
    by_rows = lambda n, w: pl.BlockSpec((n, w), lambda i: (i, 0))
    by_cols = lambda n: pl.BlockSpec((D, n), lambda i: (0, i))
    token_spec = pl.BlockSpec((CH, BLK, D), lambda i: (0, i, 0))
    values, weights, agg, agg_t, tok_t, scores_two, fold_one, fold_two, cross = call(
        forward_kernel,
        (
            shape((NB * TOK, D), F32),
            shape((NB * TOK, HEADS), F32),
            shape((NB * AGG, D), BF16),
            shape((D, NB * AGG), BF16),
            shape((D, NB * TOK), BF16),
            shape((NB * AGG, HEADS), F32),
            shape((D, 3 * HEADS), BF16),
            shape((D, 3 * HEADS), BF16),
            shape((NB * TOK, PAIRS), F32),
        ),
        4 * 10**9,
        16 * 10**6,
        grid=(NB,),
        in_specs=[SMEM, token_spec, full, full, full, whole((1, D)), whole((1, D))],
        out_specs=(
            by_rows(TOK, D),
            by_rows(TOK, HEADS),
            by_rows(AGG, D),
            by_cols(AGG),
            by_cols(TOK),
            by_rows(AGG, HEADS),
            whole((D, 3 * HEADS)),
            whole((D, 3 * HEADS)),
            by_rows(TOK, PAIRS),
        ),
        scratch_shapes=[pltpu.VMEM((2, D, PAIRS), BF16)],
    )(table, tokens, w_value, w_key, w_key_two, query_one, query_two)
    pair_two, stats = call(
        stats_kernel,
        (shape((NB * AGG, 2 * HEADS), F32), shape((16, 48, 128), F32)),
        10**9,
        2 * 10**6,
    )(agg, cot, scores_two)
    stats, values, weights = lax.optimization_barrier((stats, values, weights))
    stats = lax.all_to_all(stats, "chan", 0, 0, tiled=True)
    core = lax.rem(lax.axis_index("patch"), 2).astype(jnp.int32).reshape(1)
    weights = call(
        pre_kernel, shape((NB * TOK, 2 * HEADS), F32), 10**9, 5 * 10**6
    )(values, cot, weights)
    totals = call(total_kernel, shape((48, 128), F32), 10**6, 10**6, 4)(stats)
    fetched = (cot, pair_two, weights, fold_two, tok_t, cross, agg_t, w_key, w_key_two)
    value_grad, score_grad, send, extra = call(
        back_kernel,
        (
            shape((NB * TOK, D), BF16),
            shape((NB * TOK, HEADS), F32),
            shape((16, SLAB, 512), BF16),
            shape((8, 8, 512), F32),
        ),
        4 * 10**9,
        16 * 10**6,
        in_specs=[SMEM, SMEM, vmem] + [hbm] * len(fetched),
        out_specs=(hbm, hbm, hbm, vmem),
        scratch_shapes=[pltpu.VMEM(x.shape, x.dtype) for x in fetched]
        + [
            pltpu.VMEM((NB * TOK, D), BF16),
            pltpu.VMEM((16, SLAB, 512), BF16),
            pltpu.VMEM((NB * TOK, HEADS), F32),
            pltpu.SemaphoreType.DMA((12,)),
        ],
    )(table, core, totals, *fetched)
    got = lax.ppermute(send, "patch", [(i, i ^ 1) for i in range(16)])
    keep = call(
        keep_kernel,
        shape((16, SLAB, 512), F32),
        10**9,
        5 * 10**6,
        16,
        in_specs=[SMEM, vmem, vmem, vmem],
    )(core, tok_t, value_grad, extra)
    slabs = pl.BlockSpec((4, SLAB, 512), lambda i: (i, 0, 0))
    pairs = call(
        pair_kernel,
        shape((16, SLAB, 512), BF16),
        10**6,
        5 * 10**6,
        12,
        grid=(4,),
        in_specs=[slabs, slabs],
        out_specs=slabs,
    )(keep, got)
    planes = [
        [(2 * z + h) * 16 + 2 * k + core_bit for h in range(2) for k in range(8)]
        for z in range(8)
        for core_bit in range(2)
    ]
    got = lax.all_to_all(
        pairs, ("chan", "patch"), 0, 0, tiled=True, axis_index_groups=planes
    )
    token_grad = call(
        token_kernel,
        shape((CH, ROWS, D), BF16),
        2 * 10**9,
        6 * 10**6,
        24,
        grid=(NB,),
        in_specs=[by_rows(TOK, D), by_rows(TOK, HEADS), full, whole((D, 3 * HEADS))],
        out_specs=token_spec,
    )(value_grad, score_grad, w_value, fold_one)
    rows = call(rows_kernel, shape((8, 8, D), BF16), 10**6, 2 * 10**6, 8)(got)
    same_half = [[2 * z + h for z in range(8)] for h in range(2)]
    rows = lax.all_to_all(rows, "chan", 0, 0, tiled=True, axis_index_groups=same_half)
    rows, extra = call(
        chans_kernel, (shape((16, 8, 512), BF16), shape((8, 512), F32)), 10**6, 10**6, 8
    )(rows)
    rows = lax.all_to_all(rows, "chan", 0, 0, tiled=True)
    grad_value = call(last_kernel, shape((64, D), F32), 10**6, 10**6, 8)(rows)
    grad_key, grad_key_two, line_one, line_two = call(
        small_kernel,
        (shape((64, D), F32), shape((64, D), F32), shape((1, D), F32), shape((1, D), F32)),
        10**8,
        10**6,
        8,
    )(extra, query_one, query_two)
    return (
        token_grad,
        grad_key,
        grad_value,
        grad_key_two,
        line_one.reshape(D),
        line_two.reshape(D),
    )


def solution(mesh):
    return jax.shard_map(
        shards,
        mesh=mesh,
        in_specs=(
            P("chan", "patch", None),
            P("chan"),
            P(),
            P(),
            P(),
            P(),
            P(),
            P("patch", "chan", None),
        ),
        out_specs=(
            P("chan", "patch", None),
            P("patch", None),
            P("patch", None),
            P("patch", None),
            P(),
            P(),
        ),
        check_vma=False,
    )
```

```python
import functools

import jax
import jax.numpy as jnp
from jax import lax
from jax.experimental import pallas as pl
from jax.experimental.pallas import tpu as pltpu
from jax.sharding import PartitionSpec as P

D = 1024
HEADS = 16
HD = 64
SHIFT = 6
SCALE = 0.125
CH = 4
GR = 2
ROWS = 192
BLK = 64
NB = ROWS // BLK
TOK = CH * BLK
AGG = GR * BLK
PAIRS = HEADS * HEADS
SLAB = 72
F32 = jnp.float32
BF16 = jnp.bfloat16
MIB = 2**20


def nn(a, b):
    return lax.dot_general(a, b, (((1,), (0,)), ((), ())), preferred_element_type=F32)


def nt(a, b):
    return lax.dot_general(a, b, (((1,), (1,)), ((), ())), preferred_element_type=F32)


def split2(x):
    high = x.astype(BF16)
    return high, (x - high.astype(F32)).astype(BF16)


def split3(x):
    high = x.astype(BF16)
    rest = x - high.astype(F32)
    middle = rest.astype(BF16)
    return high, middle, (rest - middle.astype(F32)).astype(BF16)


def spread(copies):
    row = lax.broadcasted_iota(jnp.int32, (copies * HEADS, D), 0) & (HEADS - 1)
    col = lax.broadcasted_iota(jnp.int32, (copies * HEADS, D), 1) >> SHIFT
    return jnp.where(row == col, 1.0, 0.0).astype(BF16)


def expand(x, heads2):
    return nn(jnp.concatenate(split2(x), 1), heads2)


def head_sum(x, heads):
    high, low = split2(x)
    return nt(high, heads) + nt(low, heads)


def fold(weight, query):
    parts = [p.astype(F32) for p in split3(query * SCALE)]
    row = lax.broadcasted_iota(jnp.int32, (HEADS, D), 0)
    col = lax.broadcasted_iota(jnp.int32, (HEADS, D), 1) >> SHIFT
    wide = [jnp.where(row == col, p, 0.0).astype(BF16) for p in parts]
    out = nt(weight, jnp.concatenate(wide, 0))
    total = out[:, :HEADS] + out[:, HEADS : 2 * HEADS] + out[:, 2 * HEADS :]
    return jnp.concatenate(split3(total), 1)


def folded_dot(x, folded):
    out = nn(x, folded)
    return out[:, :HEADS] + out[:, HEADS : 2 * HEADS] + out[:, 2 * HEADS :]


def folded_back(x, folded):
    high, low = split2(x)
    right = jnp.concatenate(
        [folded[:, :HEADS], folded[:, HEADS : 2 * HEADS], folded[:, :HEADS]], 1
    )
    return nt(jnp.concatenate([high, high, low], 1), right)


def forward_kernel(
    table, tok, w_value, w_key, w_key_two, query_one, query_two,
    values, weights, agg, agg_t, tok_t, scores_two, fold_one, fold_two, cross,
    wide,
):
    @pl.when(pl.program_id(0) == 0)
    def _():
        fold_one[...] = fold(w_key[...], query_one[...])
        fold_two[...] = fold(w_key_two[...], query_two[...])
        row = lax.broadcasted_iota(jnp.int32, (HEADS, PAIRS), 0)
        col = lax.broadcasted_iota(jnp.int32, (HEADS, PAIRS), 1)
        copies = jnp.where(row == (col & (HEADS - 1)), 1.0, 0.0).astype(BF16)
        own = (lax.broadcasted_iota(jnp.int32, (D, PAIRS), 0) >> SHIFT) == (
            lax.broadcasted_iota(jnp.int32, (D, PAIRS), 1) >> 4
        )
        for k in range(2):
            spot = nn(fold_two[:, k * HEADS : (k + 1) * HEADS], copies)
            wide[k] = jnp.where(own, spot, 0.0).astype(BF16)

    flat = tok[...].reshape(TOK, D)
    tok_t[...] = flat.T
    scores = folded_dot(flat, fold_one[...])
    vals = nn(flat, w_value[...])
    values[...] = vals
    high, low = split2(vals)
    cross[...] = nn(high, wide[0]) + nn(high, wide[1]) + nn(low, wide[0])
    group = [table[c] for c in range(CH)]
    score = [scores[c * BLK : (c + 1) * BLK] for c in range(CH)]
    top = [
        functools.reduce(
            jnp.maximum, [jnp.where(group[c] == g, score[c], -jnp.inf) for c in range(CH)]
        )
        for g in range(GR)
    ]
    expo = [jnp.exp(score[c] - jnp.where(group[c] == 0, top[0], top[1])) for c in range(CH)]
    total = [sum(jnp.where(group[c] == g, expo[c], 0.0) for c in range(CH)) for g in range(GR)]
    weight = jnp.concatenate(
        [expo[c] / jnp.where(group[c] == 0, total[0], total[1]) for c in range(CH)], 0
    )
    weights[...] = weight
    mixed = expand(weight, spread(2)) * vals
    part = [mixed[c * BLK : (c + 1) * BLK] for c in range(CH)]
    both = jnp.concatenate(
        [sum(jnp.where(group[c] == g, part[c], 0.0) for c in range(CH)) for g in range(GR)], 0
    ).astype(BF16)
    agg[...] = both
    agg_t[...] = both.T
    scores_two[...] = folded_dot(both, fold_two[...])


def pack(x):
    return jnp.concatenate([x[24 * k : 24 * k + 24] for k in range(8)], 1)


def unpack(x):
    return jnp.concatenate([x[:, HEADS * k : HEADS * (k + 1)] for k in range(8)], 0)


def tile_kernel(cot, out):
    for k in range(16):
        out[k] = cot[0]


def stats_kernel(agg, cot, scores_two, pair_two, stats):
    heads = spread(1)
    score, grad = [[], []], [[], []]
    for b in range(NB):
        cot_f = cot[b * BLK : (b + 1) * BLK].astype(F32)
        for g in range(GR):
            rows = slice(b * AGG + g * BLK, b * AGG + (g + 1) * BLK)
            dw = head_sum(agg[rows].astype(F32) * cot_f, heads)
            grad[g].append(dw)
            score[g].append(scores_two[rows])
            pair_two[rows] = jnp.concatenate([score[g][-1], dw], 1)
    score = [jnp.concatenate(s, 0) for s in score]
    grad = [jnp.concatenate(s, 0) for s in grad]
    top = jnp.maximum(score[0], score[1])
    expo = [jnp.exp(s - top) for s in score]
    total = expo[0] + expo[1]
    log_total = top + jnp.log(total)
    inner = (expo[0] * grad[0] + expo[1] * grad[1]) / total
    both = jnp.concatenate([pack(log_total), pack(inner)], 0)
    for k in range(16):
        stats[k] = both


def pre_kernel(values, cot, weights, direct):
    heads = spread(1)
    for b in range(NB):
        trows = slice(b * TOK, (b + 1) * TOK)
        cot_f = cot[b * BLK : (b + 1) * BLK].astype(F32)
        direct[trows] = jnp.concatenate(
            [weights[trows], head_sum(jnp.concatenate([cot_f] * CH, 0) * values[trows], heads)], 1
        )


def total_kernel(stats, out):
    logs = stats[:, :24, :]
    top = jnp.max(logs, 0)
    expo = jnp.exp(logs - top[None])
    total = jnp.sum(expo, 0)
    out[:24] = top + jnp.log(total)
    out[24:] = jnp.sum(expo * stats[:, 24:, :], 0) / total


def back_kernel(
    table, core, totals_h, cot_h, pair_h, weights_h, fold_h, tok_h, cross_h, agg_h, key_h, key_two_h,
    value_grad, score_grad_h, send_h, extra_h,
    totals, cot, pair_two, weights, fold_two, tok_t, cross, agg_t, w_key, w_key_two,
    grad, send, score_grad, extra, sems,
):
    sources = (cot_h, pair_h, weights_h, fold_h, tok_h, cross_h, agg_h, key_h, key_two_h)
    targets = (cot, pair_two, weights, fold_two, tok_t, cross, agg_t, w_key, w_key_two)
    copies = [
        pltpu.make_async_copy(x, y, sems.at[k]) for k, (x, y) in enumerate(zip(sources, targets))
    ]
    first = pltpu.make_async_copy(totals_h, totals, sems.at[12])
    first.start()
    for c in copies[:5]:
        c.start()
    heads, heads2 = spread(1), spread(2)
    group = [table[c] for c in range(CH)]

    def by_channel(x):
        return jnp.concatenate(
            [jnp.where(group[c] == 0, x[:BLK], x[BLK:]) for c in range(CH)], 0
        )

    first.wait()
    log_total, inner = unpack(totals[:24]), unpack(totals[24:])
    for c in copies[:4]:
        c.wait()
    for c in copies[5:]:
        c.start()
    w_two, s_two = [], []
    for b in range(NB):
        rows = slice(b * BLK, (b + 1) * BLK)
        arows = slice(b * AGG, (b + 1) * AGG)
        trows = slice(b * TOK, (b + 1) * TOK)
        twice = lambda x: jnp.concatenate([x, x], 0)
        w_now = jnp.exp(pair_two[arows, :HEADS] - twice(log_total[rows]))
        s_now = w_now * (pair_two[arows, HEADS:] - twice(inner[rows]))
        w_two.append(w_now)
        s_two.append(s_now)
        cot_f = cot[rows].astype(F32)
        agg_grad = expand(w_now, heads2) * twice(cot_f) + folded_back(s_now, fold_two[...])
        weight = weights[trows, :HEADS]
        grad[trows] = (expand(weight, heads2) * by_channel(agg_grad)).astype(BF16)
    started = [pltpu.make_async_copy(grad, value_grad, sems.at[9])]
    started[0].start()
    copies[4].wait()
    copies[5].wait()
    row = lax.broadcasted_iota(jnp.int32, (2 * HEADS, PAIRS), 0) & (HEADS - 1)
    col = lax.broadcasted_iota(jnp.int32, (2 * HEADS, PAIRS), 1)
    tiled = jnp.where(row == (col & (HEADS - 1)), 1.0, 0.0).astype(BF16)
    gather = jnp.where(row == (col >> 4), 1.0, 0.0).astype(BF16)[:HEADS]
    for b in range(NB):
        trows = slice(b * TOK, (b + 1) * TOK)
        score = by_channel(s_two[b])
        product = nn(jnp.concatenate(split2(score), 1), tiled) * cross[trows]
        high, low = split2(product)
        direct = weights[trows, HEADS:]
        dw = by_channel(w_two[b]) * direct + nt(high, gather) + nt(low, gather)
        weight = weights[trows, :HEADS]
        wdw = weight * dw
        part = [wdw[c * BLK : (c + 1) * BLK] for c in range(CH)]
        own = jnp.concatenate(
            [sum(jnp.where(group[c] == g, part[c], 0.0) for c in range(CH)) for g in range(GR)], 0
        )
        score_grad[trows] = weight * (dw - by_channel(own))

    def outer(left, right):
        right = jnp.concatenate([right, jnp.zeros((right.shape[0], 128 - HEADS), F32)], 1).T
        both = nt(jnp.concatenate(split2(right[:HEADS]), 0), left)
        return both[:HEADS] + both[HEADS:]

    ones = outer(tok_t[...], score_grad[...])
    copies[6].wait()
    twos = outer(agg_t[...], jnp.concatenate(s_two, 0))
    grads = jnp.concatenate([ones, twos], 0)
    copies[7].wait()
    copies[8].wait()
    started.append(pltpu.make_async_copy(score_grad, score_grad_h, sems.at[10]))
    started[-1].start()
    lines = []
    for k, weight in enumerate((w_key, w_key_two)):
        high, low = split2(grads[k * HEADS : (k + 1) * HEADS])
        out = nn(jnp.concatenate([high, low], 0), weight[...])
        out = (out[:HEADS] + out[HEADS:]) * heads.astype(F32)
        lines.append(jnp.sum(out, 0, keepdims=True) * SCALE)
    quarters = jnp.concatenate(
        [line[:, k * 256 : (k + 1) * 256] for line in lines for k in range(4)], 0
    )
    left = (lax.broadcasted_iota(jnp.int32, (8, D), 1) & 64) == 0
    even, odd = [], []
    for k in range(2):
        one, two = grads[16 * k : 16 * k + 8], grads[16 * k + 8 : 16 * k + 16]
        even.append(jnp.where(left, one, jnp.concatenate([two[:, D - 64 :], two[:, : D - 64]], 1)))
        odd.append(jnp.where(left, jnp.concatenate([one[:, 64:], one[:, :64]], 1), two))
    mine = core[0]
    here = [jnp.where(mine == 0, x, y) for x, y in zip(even, odd)]
    away = [jnp.where(mine == 0, y, x) for x, y in zip(even, odd)]

    def small(pair, k):
        lanes = slice(k * 128, (k + 1) * 128)
        return jnp.concatenate([pair[0][:, lanes], pair[1][:, lanes], quarters], 1)

    for k in range(0, 8, 4):
        out = nn(peer_rows(tok_t, k, 1 - mine), grad[...])
        for i in range(4):
            extra[k + i] = small(here, k + i)
            other = small(away, k + i)
            for half in range(2):
                part = out[64 * i : 64 * (i + 1), half * 512 : (half + 1) * 512]
                send[8 * half + k + i] = jnp.concatenate([part, other], 0).astype(BF16)
    started.append(pltpu.make_async_copy(send, send_h, sems.at[11]))
    started.append(pltpu.make_async_copy(extra, extra_h, sems.at[13]))
    for c in started[-2:]:
        c.start()
    for c in started:
        c.wait()


def peer_rows(tok_t, k, side):
    return jnp.concatenate(
        [tok_t[pl.ds(pl.multiple_of((2 * (k + i) + side) * 64, 64), 64), :] for i in range(4)], 0
    )


def keep_kernel(core, tok_t, value_grad, extra, keep):
    mine = core[0]
    for k in range(0, 8, 4):
        out = nn(peer_rows(tok_t, k, mine), value_grad[...])
        for i in range(4):
            for half in range(2):
                part = out[64 * i : 64 * (i + 1), half * 512 : (half + 1) * 512]
                keep[8 * half + k + i] = jnp.concatenate([part, extra[k + i]], 0)


def pair_kernel(keep, got, out):
    out[...] = (keep[...] + got[...].astype(F32)).astype(BF16)


def token_kernel(value_grad, score_grad, w_value, fold_one, out):
    grad = nt(value_grad[...], w_value[...]) + folded_back(score_grad[...], fold_one[...])
    out[...] = grad.astype(BF16).reshape(CH, BLK, D)


def rows_kernel(got, out):
    total = got[0].astype(F32)
    for k in range(1, 16):
        total = total + got[k].astype(F32)
    total = total.astype(BF16)
    for z in range(8):
        out[z] = jnp.concatenate([total[8 * z : 8 * z + 8], total[64:]], 1)


def chans_kernel(got, rows, extra):
    total = got[0].astype(F32)
    for k in range(1, 8):
        total = total + got[k].astype(F32)
    own = total[:, :512].astype(BF16)
    for c in range(16):
        rows[c] = own
    extra[...] = total[:, 512:]


def last_kernel(got, out):
    for r in range(8):
        for half in range(2):
            out[8 * r : 8 * r + 8, half * 512 : (half + 1) * 512] = got[2 * r + half].astype(F32)


def small_kernel(extra, query_one, query_two, grad_key, grad_key_two, line_one, line_two):
    x = extra[...]
    grads = jnp.concatenate([x[:, k * 64 : (k + 1) * 64] for k in range(4)], 0)
    grads = jnp.concatenate([grads, jnp.zeros((96, 64), F32)], 0)
    turned = jnp.concatenate([grads, jnp.zeros((128, 64), F32)], 1).T[:64]
    heads3 = spread(3)
    for k, (query, out) in enumerate(((query_one, grad_key), (query_two, grad_key_two))):
        part = turned[:, k * HEADS : (k + 1) * HEADS]
        out[...] = nn(jnp.concatenate(split3(part), 1), heads3) * (query[...] * SCALE)
    for k in range(4):
        cols = slice(k * 256, (k + 1) * 256)
        line_one[:, cols] = x[k : k + 1, 256:]
        line_two[:, cols] = x[4 + k : 5 + k, 256:]


def shape(dims, dtype):
    return jax.ShapeDtypeStruct(dims, dtype)


SMEM = pl.BlockSpec(memory_space=pltpu.SMEM)


def whole(dims):
    return pl.BlockSpec(dims, lambda i: (0,) * len(dims))


def call(kernel, out_shape, flops, nbytes, limit=60, **kw):
    return pl.pallas_call(
        kernel,
        out_shape=out_shape,
        compiler_params=pltpu.CompilerParams(vmem_limit_bytes=int(limit * MIB)),
        cost_estimate=pl.CostEstimate(flops=flops, bytes_accessed=nbytes, transcendentals=0),
        **kw,
    )


def shards(tokens, table, w_key, w_value, query_one, w_key_two, query_two, cotangent):
    query_one, query_two = query_one.reshape(1, D), query_two.reshape(1, D)
    vmem = pl.BlockSpec(memory_space=pltpu.VMEM)
    hbm = pl.BlockSpec(memory_space=pltpu.HBM)
    tiled = call(
        tile_kernel,
        shape((16, ROWS // 16, D), BF16),
        10**4,
        10**6,
    )(cotangent)
    cot = lax.all_to_all(tiled, "chan", 0, 0, tiled=True).reshape(ROWS, D)
    full = whole((D, D))
    by_rows = lambda n, w: pl.BlockSpec((n, w), lambda i: (i, 0))
    by_cols = lambda n: pl.BlockSpec((D, n), lambda i: (0, i))
    token_spec = pl.BlockSpec((CH, BLK, D), lambda i: (0, i, 0))
    values, weights, agg, agg_t, tok_t, scores_two, fold_one, fold_two, cross = call(
        forward_kernel,
        (
            shape((NB * TOK, D), F32),
            shape((NB * TOK, HEADS), F32),
            shape((NB * AGG, D), BF16),
            shape((D, NB * AGG), BF16),
            shape((D, NB * TOK), BF16),
            shape((NB * AGG, HEADS), F32),
            shape((D, 3 * HEADS), BF16),
            shape((D, 3 * HEADS), BF16),
            shape((NB * TOK, PAIRS), F32),
        ),
        4 * 10**9,
        16 * 10**6,
        grid=(NB,),
        in_specs=[SMEM, token_spec, full, full, full, whole((1, D)), whole((1, D))],
        out_specs=(
            by_rows(TOK, D),
            by_rows(TOK, HEADS),
            by_rows(AGG, D),
            by_cols(AGG),
            by_cols(TOK),
            by_rows(AGG, HEADS),
            whole((D, 3 * HEADS)),
            whole((D, 3 * HEADS)),
            by_rows(TOK, PAIRS),
        ),
        scratch_shapes=[pltpu.VMEM((2, D, PAIRS), BF16)],
    )(table, tokens, w_value, w_key, w_key_two, query_one, query_two)
    pair_two, stats = call(
        stats_kernel,
        (shape((NB * AGG, 2 * HEADS), F32), shape((16, 48, 128), F32)),
        10**9,
        2 * 10**6,
    )(agg, cot, scores_two)
    stats, values, weights = lax.optimization_barrier((stats, values, weights))
    stats = lax.all_to_all(stats, "chan", 0, 0, tiled=True)
    core = lax.rem(lax.axis_index("patch"), 2).astype(jnp.int32).reshape(1)
    weights = call(
        pre_kernel, shape((NB * TOK, 2 * HEADS), F32), 10**9, 5 * 10**6
    )(values, cot, weights)
    totals = call(total_kernel, shape((48, 128), F32), 10**6, 10**6, 4)(stats)
    fetched = (cot, pair_two, weights, fold_two, tok_t, cross, agg_t, w_key, w_key_two)
    value_grad, score_grad, send, extra = call(
        back_kernel,
        (
            shape((NB * TOK, D), BF16),
            shape((NB * TOK, HEADS), F32),
            shape((16, SLAB, 512), BF16),
            shape((8, 8, 512), F32),
        ),
        4 * 10**9,
        16 * 10**6,
        53.7,
        in_specs=[SMEM, SMEM] + [hbm] * (1 + len(fetched)),
        out_specs=(hbm, hbm, hbm, hbm),
        scratch_shapes=[pltpu.VMEM(x.shape, x.dtype) for x in (totals,) + fetched]
        + [
            pltpu.VMEM((NB * TOK, D), BF16),
            pltpu.VMEM((16, SLAB, 512), BF16),
            pltpu.VMEM((NB * TOK, HEADS), F32),
            pltpu.VMEM((8, 8, 512), F32),
            pltpu.SemaphoreType.DMA((14,)),
        ],
    )(table, core, totals, *fetched)
    got = lax.ppermute(send, "patch", [(i, i ^ 1) for i in range(16)])
    keep = call(
        keep_kernel,
        shape((16, SLAB, 512), F32),
        10**9,
        5 * 10**6,
        16,
        in_specs=[SMEM, vmem, vmem, vmem],
    )(core, tok_t, value_grad, extra)
    slabs = pl.BlockSpec((4, SLAB, 512), lambda i: (i, 0, 0))
    pairs = call(
        pair_kernel,
        shape((16, SLAB, 512), BF16),
        10**6,
        5 * 10**6,
        12,
        grid=(4,),
        in_specs=[slabs, slabs],
        out_specs=slabs,
    )(keep, got)
    planes = [
        [(2 * z + h) * 16 + 2 * k + core_bit for h in range(2) for k in range(8)]
        for z in range(8)
        for core_bit in range(2)
    ]
    got = lax.all_to_all(
        pairs, ("chan", "patch"), 0, 0, tiled=True, axis_index_groups=planes
    )
    token_grad = call(
        token_kernel,
        shape((CH, ROWS, D), BF16),
        2 * 10**9,
        6 * 10**6,
        24,
        grid=(NB,),
        in_specs=[by_rows(TOK, D), by_rows(TOK, HEADS), full, whole((D, 3 * HEADS))],
        out_specs=token_spec,
    )(value_grad, score_grad, w_value, fold_one)
    rows = call(rows_kernel, shape((8, 8, D), BF16), 10**6, 2 * 10**6, 8)(got)
    same_half = [[2 * z + h for z in range(8)] for h in range(2)]
    rows = lax.all_to_all(rows, "chan", 0, 0, tiled=True, axis_index_groups=same_half)
    rows, extra = call(
        chans_kernel, (shape((16, 8, 512), BF16), shape((8, 512), F32)), 10**6, 10**6, 8
    )(rows)
    rows = lax.all_to_all(rows, "chan", 0, 0, tiled=True)
    grad_value = call(last_kernel, shape((64, D), F32), 10**6, 10**6, 8)(rows)
    grad_key, grad_key_two, line_one, line_two = call(
        small_kernel,
        (shape((64, D), F32), shape((64, D), F32), shape((1, D), F32), shape((1, D), F32)),
        10**8,
        10**6,
        8,
    )(extra, query_one, query_two)
    return (
        token_grad,
        grad_key,
        grad_value,
        grad_key_two,
        line_one.reshape(D),
        line_two.reshape(D),
    )


def solution(mesh):
    return jax.shard_map(
        shards,
        mesh=mesh,
        in_specs=(
            P("chan", "patch", None),
            P("chan"),
            P(),
            P(),
            P(),
            P(),
            P(),
            P("patch", "chan", None),
        ),
        out_specs=(
            P("chan", "patch", None),
            P("patch", None),
            P("patch", None),
            P("patch", None),
            P(),
            P(),
        ),
        check_vma=False,
    )
```

```python
import functools

import jax
import jax.numpy as jnp
from jax import lax
from jax.experimental import pallas as pl
from jax.experimental.pallas import tpu as pltpu
from jax.sharding import PartitionSpec as P

D = 1024
HEADS = 16
HD = 64
SHIFT = 6
SCALE = 0.125
CH = 4
GR = 2
ROWS = 192
BLK = 64
NB = ROWS // BLK
TOK = CH * BLK
AGG = GR * BLK
PAIRS = HEADS * HEADS
SLAB = 72
F32 = jnp.float32
BF16 = jnp.bfloat16
MIB = 2**20


def nn(a, b):
    return lax.dot_general(a, b, (((1,), (0,)), ((), ())), preferred_element_type=F32)


def nt(a, b):
    return lax.dot_general(a, b, (((1,), (1,)), ((), ())), preferred_element_type=F32)


def split2(x):
    high = x.astype(BF16)
    return high, (x - high.astype(F32)).astype(BF16)


def split3(x):
    high = x.astype(BF16)
    rest = x - high.astype(F32)
    middle = rest.astype(BF16)
    return high, middle, (rest - middle.astype(F32)).astype(BF16)


def spread(copies):
    row = lax.broadcasted_iota(jnp.int32, (copies * HEADS, D), 0) & (HEADS - 1)
    col = lax.broadcasted_iota(jnp.int32, (copies * HEADS, D), 1) >> SHIFT
    return jnp.where(row == col, 1.0, 0.0).astype(BF16)


def expand(x, heads2):
    return nn(jnp.concatenate(split2(x), 1), heads2)


def head_sum(x, heads):
    high, low = split2(x)
    return nt(high, heads) + nt(low, heads)


def fold(weight, query):
    parts = [p.astype(F32) for p in split3(query * SCALE)]
    row = lax.broadcasted_iota(jnp.int32, (HEADS, D), 0)
    col = lax.broadcasted_iota(jnp.int32, (HEADS, D), 1) >> SHIFT
    wide = [jnp.where(row == col, p, 0.0).astype(BF16) for p in parts]
    out = nt(weight, jnp.concatenate(wide, 0))
    total = out[:, :HEADS] + out[:, HEADS : 2 * HEADS] + out[:, 2 * HEADS :]
    return jnp.concatenate(split3(total), 1)


def folded_dot(x, folded):
    out = nn(x, folded)
    return out[:, :HEADS] + out[:, HEADS : 2 * HEADS] + out[:, 2 * HEADS :]


def folded_back(x, folded):
    high, low = split2(x)
    right = jnp.concatenate(
        [folded[:, :HEADS], folded[:, HEADS : 2 * HEADS], folded[:, :HEADS]], 1
    )
    return nt(jnp.concatenate([high, high, low], 1), right)


def forward_kernel(
    table, tok, w_value, w_key, w_key_two, query_one, query_two,
    values, weights, agg, agg_t, tok_t, scores_two, fold_one, fold_two, cross,
    wide,
):
    @pl.when(pl.program_id(0) == 0)
    def _():
        fold_one[...] = fold(w_key[...], query_one[...])
        fold_two[...] = fold(w_key_two[...], query_two[...])
        row = lax.broadcasted_iota(jnp.int32, (HEADS, PAIRS), 0)
        col = lax.broadcasted_iota(jnp.int32, (HEADS, PAIRS), 1)
        copies = jnp.where(row == (col & (HEADS - 1)), 1.0, 0.0).astype(BF16)
        own = (lax.broadcasted_iota(jnp.int32, (D, PAIRS), 0) >> SHIFT) == (
            lax.broadcasted_iota(jnp.int32, (D, PAIRS), 1) >> 4
        )
        for k in range(2):
            spot = nn(fold_two[:, k * HEADS : (k + 1) * HEADS], copies)
            wide[k] = jnp.where(own, spot, 0.0).astype(BF16)

    flat = tok[...].reshape(TOK, D)
    tok_t[...] = flat.T
    scores = folded_dot(flat, fold_one[...])
    vals = nn(flat, w_value[...])
    values[...] = vals
    high, low = split2(vals)
    cross[...] = nn(high, wide[0]) + nn(high, wide[1]) + nn(low, wide[0])
    group = [table[c] for c in range(CH)]
    score = [scores[c * BLK : (c + 1) * BLK] for c in range(CH)]
    top = [
        functools.reduce(
            jnp.maximum, [jnp.where(group[c] == g, score[c], -jnp.inf) for c in range(CH)]
        )
        for g in range(GR)
    ]
    expo = [jnp.exp(score[c] - jnp.where(group[c] == 0, top[0], top[1])) for c in range(CH)]
    total = [sum(jnp.where(group[c] == g, expo[c], 0.0) for c in range(CH)) for g in range(GR)]
    weight = jnp.concatenate(
        [expo[c] / jnp.where(group[c] == 0, total[0], total[1]) for c in range(CH)], 0
    )
    weights[...] = weight
    mixed = expand(weight, spread(2)) * vals
    part = [mixed[c * BLK : (c + 1) * BLK] for c in range(CH)]
    both = jnp.concatenate(
        [sum(jnp.where(group[c] == g, part[c], 0.0) for c in range(CH)) for g in range(GR)], 0
    ).astype(BF16)
    agg[...] = both
    agg_t[...] = both.T
    scores_two[...] = folded_dot(both, fold_two[...])


def pack(x):
    return jnp.concatenate([x[24 * k : 24 * k + 24] for k in range(8)], 1)


def unpack(x):
    return jnp.concatenate([x[:, HEADS * k : HEADS * (k + 1)] for k in range(8)], 0)


def tile_kernel(cot, out):
    for k in range(16):
        out[k] = cot[0]


def stats_kernel(agg, cot, scores_two, pair_two, stats):
    heads = spread(1)
    score, grad = [[], []], [[], []]
    for b in range(NB):
        cot_f = cot[b * BLK : (b + 1) * BLK].astype(F32)
        for g in range(GR):
            rows = slice(b * AGG + g * BLK, b * AGG + (g + 1) * BLK)
            dw = head_sum(agg[rows].astype(F32) * cot_f, heads)
            grad[g].append(dw)
            score[g].append(scores_two[rows])
            pair_two[rows] = jnp.concatenate([score[g][-1], dw], 1)
    score = [jnp.concatenate(s, 0) for s in score]
    grad = [jnp.concatenate(s, 0) for s in grad]
    top = jnp.maximum(score[0], score[1])
    expo = [jnp.exp(s - top) for s in score]
    total = expo[0] + expo[1]
    log_total = top + jnp.log(total)
    inner = (expo[0] * grad[0] + expo[1] * grad[1]) / total
    both = jnp.concatenate([pack(log_total), pack(inner)], 0)
    for k in range(16):
        stats[k] = both


def pre_kernel(values, cot, weights, direct):
    heads = spread(1)
    for b in range(NB):
        trows = slice(b * TOK, (b + 1) * TOK)
        cot_f = cot[b * BLK : (b + 1) * BLK].astype(F32)
        direct[trows] = jnp.concatenate(
            [weights[trows], head_sum(jnp.concatenate([cot_f] * CH, 0) * values[trows], heads)], 1
        )


def total_kernel(stats, out):
    logs = stats[:, :24, :]
    top = jnp.max(logs, 0)
    expo = jnp.exp(logs - top[None])
    total = jnp.sum(expo, 0)
    out[:24] = top + jnp.log(total)
    out[24:] = jnp.sum(expo * stats[:, 24:, :], 0) / total


def back_kernel(
    table, core, totals_h, cot_h, pair_h, weights_h, fold_h, tok_h, cross_h, agg_h, key_h, key_two_h,
    value_grad, score_grad_h, send_h, extra_h,
    totals, cot, pair_two, weights, fold_two, tok_t, cross, agg_t, w_key, w_key_two,
    grad, send, score_grad, score_turned, extra, sems,
):
    sources = (cot_h, pair_h, weights_h, fold_h, tok_h, cross_h, agg_h, key_h, key_two_h)
    targets = (cot, pair_two, weights, fold_two, tok_t, cross, agg_t, w_key, w_key_two)
    copies = [
        pltpu.make_async_copy(x, y, sems.at[k]) for k, (x, y) in enumerate(zip(sources, targets))
    ]
    first = pltpu.make_async_copy(totals_h, totals, sems.at[12])
    first.start()
    for c in copies[:5]:
        c.start()
    heads, heads2 = spread(1), spread(2)
    group = [table[c] for c in range(CH)]

    def by_channel(x):
        return jnp.concatenate(
            [jnp.where(group[c] == 0, x[:BLK], x[BLK:]) for c in range(CH)], 0
        )

    first.wait()
    log_total, inner = unpack(totals[:24]), unpack(totals[24:])
    for c in copies[:4]:
        c.wait()
    for c in copies[5:]:
        c.start()
    w_two, s_two = [], []
    for b in range(NB):
        rows = slice(b * BLK, (b + 1) * BLK)
        arows = slice(b * AGG, (b + 1) * AGG)
        trows = slice(b * TOK, (b + 1) * TOK)
        twice = lambda x: jnp.concatenate([x, x], 0)
        w_now = jnp.exp(pair_two[arows, :HEADS] - twice(log_total[rows]))
        s_now = w_now * (pair_two[arows, HEADS:] - twice(inner[rows]))
        w_two.append(w_now)
        s_two.append(s_now)
        cot_f = cot[rows].astype(F32)
        agg_grad = expand(w_now, heads2) * twice(cot_f) + folded_back(s_now, fold_two[...])
        weight = weights[trows, :HEADS]
        grad[trows] = (expand(weight, heads2) * by_channel(agg_grad)).astype(BF16)
    copies[4].wait()
    copies[5].wait()
    row = lax.broadcasted_iota(jnp.int32, (2 * HEADS, PAIRS), 0) & (HEADS - 1)
    col = lax.broadcasted_iota(jnp.int32, (2 * HEADS, PAIRS), 1)
    tiled = jnp.where(row == (col & (HEADS - 1)), 1.0, 0.0).astype(BF16)
    gather = jnp.where(row == (col >> 4), 1.0, 0.0).astype(BF16)[:HEADS]
    for b in range(NB):
        trows = slice(b * TOK, (b + 1) * TOK)
        score = by_channel(s_two[b])
        product = nn(jnp.concatenate(split2(score), 1), tiled) * cross[trows]
        high, low = split2(product)
        direct = weights[trows, HEADS:]
        dw = by_channel(w_two[b]) * direct + nt(high, gather) + nt(low, gather)
        weight = weights[trows, :HEADS]
        wdw = weight * dw
        part = [wdw[c * BLK : (c + 1) * BLK] for c in range(CH)]
        own = jnp.concatenate(
            [sum(jnp.where(group[c] == g, part[c], 0.0) for c in range(CH)) for g in range(GR)], 0
        )
        score_grad[trows] = weight * (dw - by_channel(own))

    def turn(x):
        return jnp.concatenate([x, jnp.zeros((x.shape[0], 128 - HEADS), F32)], 1).T[:HEADS]

    def outer(left, right):
        both = nt(jnp.concatenate(split2(right), 0), left)
        return both[:HEADS] + both[HEADS:]

    score_turned[...] = turn(score_grad[...])
    ones = outer(tok_t[...], score_turned[...])
    copies[6].wait()
    twos = outer(agg_t[...], turn(jnp.concatenate(s_two, 0)))
    grads = jnp.concatenate([ones, twos], 0)
    copies[7].wait()
    copies[8].wait()
    started = [
        pltpu.make_async_copy(grad, value_grad, sems.at[9]),
        pltpu.make_async_copy(score_turned, score_grad_h, sems.at[10]),
    ]
    for c in started:
        c.start()
    lines = []
    for k, weight in enumerate((w_key, w_key_two)):
        high, low = split2(grads[k * HEADS : (k + 1) * HEADS])
        out = nn(jnp.concatenate([high, low], 0), weight[...])
        out = (out[:HEADS] + out[HEADS:]) * heads.astype(F32)
        lines.append(jnp.sum(out, 0, keepdims=True) * SCALE)
    quarters = jnp.concatenate(
        [line[:, k * 256 : (k + 1) * 256] for line in lines for k in range(4)], 0
    )
    left = (lax.broadcasted_iota(jnp.int32, (8, D), 1) & 64) == 0
    even, odd = [], []
    for k in range(2):
        one, two = grads[16 * k : 16 * k + 8], grads[16 * k + 8 : 16 * k + 16]
        even.append(jnp.where(left, one, jnp.concatenate([two[:, D - 64 :], two[:, : D - 64]], 1)))
        odd.append(jnp.where(left, jnp.concatenate([one[:, 64:], one[:, :64]], 1), two))
    mine = core[0]
    here = [jnp.where(mine == 0, x, y) for x, y in zip(even, odd)]
    away = [jnp.where(mine == 0, y, x) for x, y in zip(even, odd)]

    def small(pair, k):
        lanes = slice(k * 128, (k + 1) * 128)
        return jnp.concatenate([pair[0][:, lanes], pair[1][:, lanes], quarters], 1)

    for k in range(0, 8, 4):
        out = nn(peer_rows(tok_t, k, 1 - mine), grad[...])
        for i in range(4):
            extra[k + i] = small(here, k + i)
            other = small(away, k + i)
            for half in range(2):
                part = out[64 * i : 64 * (i + 1), half * 512 : (half + 1) * 512]
                send[8 * half + k + i] = jnp.concatenate([part, other], 0).astype(BF16)
    started.append(pltpu.make_async_copy(send, send_h, sems.at[11]))
    started.append(pltpu.make_async_copy(extra, extra_h, sems.at[13]))
    for c in started[-2:]:
        c.start()
    for c in started:
        c.wait()


def peer_rows(tok_t, k, side):
    return jnp.concatenate(
        [tok_t[pl.ds(pl.multiple_of((2 * (k + i) + side) * 64, 64), 64), :] for i in range(4)], 0
    )


def keep_kernel(core, tok_t, value_grad, extra, keep):
    mine = core[0]
    for k in range(0, 8, 4):
        out = nn(peer_rows(tok_t, k, mine), value_grad[...])
        for i in range(4):
            for half in range(2):
                part = out[64 * i : 64 * (i + 1), half * 512 : (half + 1) * 512]
                keep[8 * half + k + i] = jnp.concatenate([part, extra[k + i]], 0)


def pair_kernel(keep, got, out):
    out[...] = (keep[...] + got[...].astype(F32)).astype(BF16)


def token_kernel(value_grad, score_grad, w_value, fold_one, out):
    grad = nt(value_grad[...], w_value[...]) + folded_back(score_grad[...].T, fold_one[...])
    out[...] = grad.astype(BF16).reshape(CH, BLK, D)


def rows_kernel(got, out):
    total = got[0].astype(F32)
    for k in range(1, 16):
        total = total + got[k].astype(F32)
    total = total.astype(BF16)
    for z in range(8):
        out[z] = jnp.concatenate([total[8 * z : 8 * z + 8], total[64:]], 1)


def chans_kernel(got, rows, extra):
    total = got[0].astype(F32)
    for k in range(1, 8):
        total = total + got[k].astype(F32)
    own = total[:, :512].astype(BF16)
    for c in range(16):
        rows[c] = own
    extra[...] = total[:, 512:]


def last_kernel(got, out):
    for r in range(8):
        for half in range(2):
            out[8 * r : 8 * r + 8, half * 512 : (half + 1) * 512] = got[2 * r + half].astype(F32)


def small_kernel(extra, query_one, query_two, grad_key, grad_key_two, line_one, line_two):
    x = extra[...]
    grads = jnp.concatenate([x[:, k * 64 : (k + 1) * 64] for k in range(4)], 0)
    grads = jnp.concatenate([grads, jnp.zeros((96, 64), F32)], 0)
    turned = jnp.concatenate([grads, jnp.zeros((128, 64), F32)], 1).T[:64]
    heads3 = spread(3)
    for k, (query, out) in enumerate(((query_one, grad_key), (query_two, grad_key_two))):
        part = turned[:, k * HEADS : (k + 1) * HEADS]
        out[...] = nn(jnp.concatenate(split3(part), 1), heads3) * (query[...] * SCALE)
    for k in range(4):
        cols = slice(k * 256, (k + 1) * 256)
        line_one[:, cols] = x[k : k + 1, 256:]
        line_two[:, cols] = x[4 + k : 5 + k, 256:]


def shape(dims, dtype):
    return jax.ShapeDtypeStruct(dims, dtype)


SMEM = pl.BlockSpec(memory_space=pltpu.SMEM)


def whole(dims):
    return pl.BlockSpec(dims, lambda i: (0,) * len(dims))


def call(kernel, out_shape, flops, nbytes, limit=60, **kw):
    return pl.pallas_call(
        kernel,
        out_shape=out_shape,
        compiler_params=pltpu.CompilerParams(vmem_limit_bytes=int(limit * MIB)),
        cost_estimate=pl.CostEstimate(flops=flops, bytes_accessed=nbytes, transcendentals=0),
        **kw,
    )


def shards(tokens, table, w_key, w_value, query_one, w_key_two, query_two, cotangent):
    query_one, query_two = query_one.reshape(1, D), query_two.reshape(1, D)
    vmem = pl.BlockSpec(memory_space=pltpu.VMEM)
    hbm = pl.BlockSpec(memory_space=pltpu.HBM)
    tiled = call(
        tile_kernel,
        shape((16, ROWS // 16, D), BF16),
        10**4,
        10**6,
    )(cotangent)
    cot = lax.all_to_all(tiled, "chan", 0, 0, tiled=True).reshape(ROWS, D)
    full = whole((D, D))
    by_rows = lambda n, w: pl.BlockSpec((n, w), lambda i: (i, 0))
    by_cols = lambda n: pl.BlockSpec((D, n), lambda i: (0, i))
    token_spec = pl.BlockSpec((CH, BLK, D), lambda i: (0, i, 0))
    values, weights, agg, agg_t, tok_t, scores_two, fold_one, fold_two, cross = call(
        forward_kernel,
        (
            shape((NB * TOK, D), F32),
            shape((NB * TOK, HEADS), F32),
            shape((NB * AGG, D), BF16),
            shape((D, NB * AGG), BF16),
            shape((D, NB * TOK), BF16),
            shape((NB * AGG, HEADS), F32),
            shape((D, 3 * HEADS), BF16),
            shape((D, 3 * HEADS), BF16),
            shape((NB * TOK, PAIRS), F32),
        ),
        4 * 10**9,
        16 * 10**6,
        grid=(NB,),
        in_specs=[SMEM, token_spec, full, full, full, whole((1, D)), whole((1, D))],
        out_specs=(
            by_rows(TOK, D),
            by_rows(TOK, HEADS),
            by_rows(AGG, D),
            by_cols(AGG),
            by_cols(TOK),
            by_rows(AGG, HEADS),
            whole((D, 3 * HEADS)),
            whole((D, 3 * HEADS)),
            by_rows(TOK, PAIRS),
        ),
        scratch_shapes=[pltpu.VMEM((2, D, PAIRS), BF16)],
    )(table, tokens, w_value, w_key, w_key_two, query_one, query_two)
    pair_two, stats = call(
        stats_kernel,
        (shape((NB * AGG, 2 * HEADS), F32), shape((16, 48, 128), F32)),
        10**9,
        2 * 10**6,
    )(agg, cot, scores_two)
    stats, values, weights = lax.optimization_barrier((stats, values, weights))
    stats = lax.all_to_all(stats, "chan", 0, 0, tiled=True)
    core = lax.rem(lax.axis_index("patch"), 2).astype(jnp.int32).reshape(1)
    weights = call(
        pre_kernel, shape((NB * TOK, 2 * HEADS), F32), 10**9, 5 * 10**6
    )(values, cot, weights)
    totals = call(total_kernel, shape((48, 128), F32), 10**6, 10**6, 4)(stats)
    fetched = (cot, pair_two, weights, fold_two, tok_t, cross, agg_t, w_key, w_key_two)
    value_grad, score_grad, send, extra = call(
        back_kernel,
        (
            shape((NB * TOK, D), BF16),
            shape((HEADS, NB * TOK), F32),
            shape((16, SLAB, 512), BF16),
            shape((8, 8, 512), F32),
        ),
        4 * 10**9,
        16 * 10**6,
        53.7,
        in_specs=[SMEM, SMEM] + [hbm] * (1 + len(fetched)),
        out_specs=(hbm, hbm, hbm, hbm),
        scratch_shapes=[pltpu.VMEM(x.shape, x.dtype) for x in (totals,) + fetched]
        + [
            pltpu.VMEM((NB * TOK, D), BF16),
            pltpu.VMEM((16, SLAB, 512), BF16),
            pltpu.VMEM((NB * TOK, HEADS), F32),
            pltpu.VMEM((HEADS, NB * TOK), F32),
            pltpu.VMEM((8, 8, 512), F32),
            pltpu.SemaphoreType.DMA((14,)),
        ],
    )(table, core, totals, *fetched)
    got = lax.ppermute(send, "patch", [(i, i ^ 1) for i in range(16)])
    keep = call(
        keep_kernel,
        shape((16, SLAB, 512), F32),
        10**9,
        5 * 10**6,
        16,
        in_specs=[SMEM, vmem, vmem, vmem],
    )(core, tok_t, value_grad, extra)
    slabs = pl.BlockSpec((4, SLAB, 512), lambda i: (i, 0, 0))
    pairs = call(
        pair_kernel,
        shape((16, SLAB, 512), BF16),
        10**6,
        5 * 10**6,
        12,
        grid=(4,),
        in_specs=[slabs, slabs],
        out_specs=slabs,
    )(keep, got)
    planes = [
        [(2 * z + h) * 16 + 2 * k + core_bit for h in range(2) for k in range(8)]
        for z in range(8)
        for core_bit in range(2)
    ]
    got = lax.all_to_all(
        pairs, ("chan", "patch"), 0, 0, tiled=True, axis_index_groups=planes
    )
    token_grad = call(
        token_kernel,
        shape((CH, ROWS, D), BF16),
        2 * 10**9,
        6 * 10**6,
        24,
        grid=(NB,),
        in_specs=[
            by_rows(TOK, D),
            pl.BlockSpec((HEADS, TOK), lambda i: (0, i)),
            full,
            whole((D, 3 * HEADS)),
        ],
        out_specs=token_spec,
    )(value_grad, score_grad, w_value, fold_one)
    rows = call(rows_kernel, shape((8, 8, D), BF16), 10**6, 2 * 10**6, 8)(got)
    same_half = [[2 * z + h for z in range(8)] for h in range(2)]
    rows = lax.all_to_all(rows, "chan", 0, 0, tiled=True, axis_index_groups=same_half)
    rows, extra = call(
        chans_kernel, (shape((16, 8, 512), BF16), shape((8, 512), F32)), 10**6, 10**6, 8
    )(rows)
    rows = lax.all_to_all(rows, "chan", 0, 0, tiled=True)
    grad_value = call(last_kernel, shape((64, D), F32), 10**6, 10**6, 8)(rows)
    grad_key, grad_key_two, line_one, line_two = call(
        small_kernel,
        (shape((64, D), F32), shape((64, D), F32), shape((1, D), F32), shape((1, D), F32)),
        10**8,
        10**6,
        8,
    )(extra, query_one, query_two)
    return (
        token_grad,
        grad_key,
        grad_value,
        grad_key_two,
        line_one.reshape(D),
        line_two.reshape(D),
    )


def solution(mesh):
    return jax.shard_map(
        shards,
        mesh=mesh,
        in_specs=(
            P("chan", "patch", None),
            P("chan"),
            P(),
            P(),
            P(),
            P(),
            P(),
            P("patch", "chan", None),
        ),
        out_specs=(
            P("chan", "patch", None),
            P("patch", None),
            P("patch", None),
            P("patch", None),
            P(),
            P(),
        ),
        check_vma=False,
    )
```

```python
import functools

import jax
import jax.numpy as jnp
from jax import lax
from jax.experimental import pallas as pl
from jax.experimental.pallas import tpu as pltpu
from jax.sharding import PartitionSpec as P

D = 1024
HEADS = 16
HD = 64
SHIFT = 6
SCALE = 0.125
CH = 4
GR = 2
ROWS = 192
BLK = 64
NB = ROWS // BLK
TOK = CH * BLK
AGG = GR * BLK
PAIRS = HEADS * HEADS
SLAB = 72
F32 = jnp.float32
BF16 = jnp.bfloat16
MIB = 2**20


def nn(a, b):
    return lax.dot_general(a, b, (((1,), (0,)), ((), ())), preferred_element_type=F32)


def nt(a, b):
    return lax.dot_general(a, b, (((1,), (1,)), ((), ())), preferred_element_type=F32)


def split2(x):
    high = x.astype(BF16)
    return high, (x - high.astype(F32)).astype(BF16)


def split3(x):
    high = x.astype(BF16)
    rest = x - high.astype(F32)
    middle = rest.astype(BF16)
    return high, middle, (rest - middle.astype(F32)).astype(BF16)


def spread(copies):
    row = lax.broadcasted_iota(jnp.int32, (copies * HEADS, D), 0) & (HEADS - 1)
    col = lax.broadcasted_iota(jnp.int32, (copies * HEADS, D), 1) >> SHIFT
    return jnp.where(row == col, 1.0, 0.0).astype(BF16)


def expand(x, heads2):
    return nn(jnp.concatenate(split2(x), 1), heads2)


def head_sum(x, heads):
    high, low = split2(x)
    return nt(high, heads) + nt(low, heads)


def fold(weight, query):
    parts = [p.astype(F32) for p in split3(query * SCALE)]
    row = lax.broadcasted_iota(jnp.int32, (HEADS, D), 0)
    col = lax.broadcasted_iota(jnp.int32, (HEADS, D), 1) >> SHIFT
    wide = [jnp.where(row == col, p, 0.0).astype(BF16) for p in parts]
    out = nt(weight, jnp.concatenate(wide, 0))
    total = out[:, :HEADS] + out[:, HEADS : 2 * HEADS] + out[:, 2 * HEADS :]
    return jnp.concatenate(split3(total), 1)


def folded_dot(x, folded):
    out = nn(x, folded)
    return out[:, :HEADS] + out[:, HEADS : 2 * HEADS] + out[:, 2 * HEADS :]


def folded_back(x, folded):
    high, low = split2(x)
    right = jnp.concatenate(
        [folded[:, :HEADS], folded[:, HEADS : 2 * HEADS], folded[:, :HEADS]], 1
    )
    return nt(jnp.concatenate([high, high, low], 1), right)


def forward_kernel(
    table, tok, w_value, w_key, w_key_two, query_one, query_two,
    values, weights, agg, agg_t, tok_t, scores_two, fold_one, fold_two, cross,
    wide,
):
    @pl.when(pl.program_id(0) == 0)
    def _():
        fold_one[...] = fold(w_key[...], query_one[...])
        fold_two[...] = fold(w_key_two[...], query_two[...])
        row = lax.broadcasted_iota(jnp.int32, (HEADS, PAIRS), 0)
        col = lax.broadcasted_iota(jnp.int32, (HEADS, PAIRS), 1)
        copies = jnp.where(row == (col & (HEADS - 1)), 1.0, 0.0).astype(BF16)
        own = (lax.broadcasted_iota(jnp.int32, (D, PAIRS), 0) >> SHIFT) == (
            lax.broadcasted_iota(jnp.int32, (D, PAIRS), 1) >> 4
        )
        for k in range(2):
            spot = nn(fold_two[:, k * HEADS : (k + 1) * HEADS], copies)
            wide[k] = jnp.where(own, spot, 0.0).astype(BF16)

    flat = tok[...].reshape(TOK, D)
    tok_t[...] = flat.T
    scores = folded_dot(flat, fold_one[...])
    vals = nn(flat, w_value[...])
    values[...] = vals
    high, low = split2(vals)
    cross[...] = nn(high, wide[0]) + nn(high, wide[1]) + nn(low, wide[0])
    group = [table[c] for c in range(CH)]
    score = [scores[c * BLK : (c + 1) * BLK] for c in range(CH)]
    top = [
        functools.reduce(
            jnp.maximum, [jnp.where(group[c] == g, score[c], -jnp.inf) for c in range(CH)]
        )
        for g in range(GR)
    ]
    expo = [jnp.exp(score[c] - jnp.where(group[c] == 0, top[0], top[1])) for c in range(CH)]
    total = [sum(jnp.where(group[c] == g, expo[c], 0.0) for c in range(CH)) for g in range(GR)]
    weight = jnp.concatenate(
        [expo[c] / jnp.where(group[c] == 0, total[0], total[1]) for c in range(CH)], 0
    )
    weights[...] = weight
    mixed = expand(weight, spread(2)) * vals
    part = [mixed[c * BLK : (c + 1) * BLK] for c in range(CH)]
    both = jnp.concatenate(
        [sum(jnp.where(group[c] == g, part[c], 0.0) for c in range(CH)) for g in range(GR)], 0
    ).astype(BF16)
    agg[...] = both
    agg_t[...] = both.T
    scores_two[...] = folded_dot(both, fold_two[...])


def pack(x):
    return jnp.concatenate([x[24 * k : 24 * k + 24] for k in range(8)], 1)


def unpack(x):
    return jnp.concatenate([x[:, HEADS * k : HEADS * (k + 1)] for k in range(8)], 0)


def tile_kernel(cot, out):
    for k in range(16):
        out[k] = cot[0]


def stats_kernel(agg, cot, scores_two, pair_two, stats):
    heads = spread(1)
    score, grad = [[], []], [[], []]
    for b in range(NB):
        cot_f = cot[b * BLK : (b + 1) * BLK].astype(F32)
        for g in range(GR):
            rows = slice(b * AGG + g * BLK, b * AGG + (g + 1) * BLK)
            dw = head_sum(agg[rows].astype(F32) * cot_f, heads)
            grad[g].append(dw)
            score[g].append(scores_two[rows])
            pair_two[rows] = jnp.concatenate([score[g][-1], dw], 1)
    score = [jnp.concatenate(s, 0) for s in score]
    grad = [jnp.concatenate(s, 0) for s in grad]
    top = jnp.maximum(score[0], score[1])
    expo = [jnp.exp(s - top) for s in score]
    total = expo[0] + expo[1]
    log_total = top + jnp.log(total)
    inner = (expo[0] * grad[0] + expo[1] * grad[1]) / total
    both = jnp.concatenate([pack(log_total), pack(inner)], 0)
    for k in range(16):
        stats[k] = both


def pre_kernel(values, cot, weights, direct):
    heads = spread(1)
    for b in range(NB):
        trows = slice(b * TOK, (b + 1) * TOK)
        cot_f = cot[b * BLK : (b + 1) * BLK].astype(F32)
        direct[trows] = jnp.concatenate(
            [weights[trows], head_sum(jnp.concatenate([cot_f] * CH, 0) * values[trows], heads)], 1
        )


def total_kernel(stats, out):
    logs = stats[:, :24, :]
    top = jnp.max(logs, 0)
    expo = jnp.exp(logs - top[None])
    total = jnp.sum(expo, 0)
    out[:24] = top + jnp.log(total)
    out[24:] = jnp.sum(expo * stats[:, 24:, :], 0) / total


def back_kernel(
    table, core, totals_h, cot_h, pair_h, weights_h, fold_h, tok_h, cross_h, agg_h, key_h, key_two_h,
    value_grad, score_grad_h, send_h, extra_h,
    totals, cot, pair_two, weights, fold_two, tok_t, cross, agg_t, w_key, w_key_two,
    grad, send, score_grad, score_turned, extra, sems,
):
    sources = (cot_h, pair_h, weights_h, fold_h, tok_h, cross_h, agg_h, key_h, key_two_h)
    targets = (cot, pair_two, weights, fold_two, tok_t, cross, agg_t, w_key, w_key_two)
    copies = [
        pltpu.make_async_copy(x, y, sems.at[k]) for k, (x, y) in enumerate(zip(sources, targets))
    ]
    first = pltpu.make_async_copy(totals_h, totals, sems.at[12])
    first.start()
    for c in copies[:5]:
        c.start()
    heads, heads2 = spread(1), spread(2)
    group = [table[c] for c in range(CH)]

    def by_channel(x):
        return jnp.concatenate(
            [jnp.where(group[c] == 0, x[:BLK], x[BLK:]) for c in range(CH)], 0
        )

    first.wait()
    log_total, inner = unpack(totals[:24]), unpack(totals[24:])
    for c in copies[:4]:
        c.wait()
    for c in copies[5:]:
        c.start()
    w_two, s_two = [], []
    for b in range(NB):
        rows = slice(b * BLK, (b + 1) * BLK)
        arows = slice(b * AGG, (b + 1) * AGG)
        trows = slice(b * TOK, (b + 1) * TOK)
        twice = lambda x: jnp.concatenate([x, x], 0)
        w_now = jnp.exp(pair_two[arows, :HEADS] - twice(log_total[rows]))
        s_now = w_now * (pair_two[arows, HEADS:] - twice(inner[rows]))
        w_two.append(w_now)
        s_two.append(s_now)
        cot_f = cot[rows].astype(F32)
        agg_grad = expand(w_now, heads2) * twice(cot_f) + folded_back(s_now, fold_two[...])
        weight = weights[trows, :HEADS]
        grad[trows] = (expand(weight, heads2) * by_channel(agg_grad)).astype(BF16)
    copies[4].wait()
    copies[5].wait()
    row = lax.broadcasted_iota(jnp.int32, (2 * HEADS, PAIRS), 0) & (HEADS - 1)
    col = lax.broadcasted_iota(jnp.int32, (2 * HEADS, PAIRS), 1)
    tiled = jnp.where(row == (col & (HEADS - 1)), 1.0, 0.0).astype(BF16)
    gather = jnp.where(row == (col >> 4), 1.0, 0.0).astype(BF16)[:HEADS]
    for b in range(NB):
        trows = slice(b * TOK, (b + 1) * TOK)
        score = by_channel(s_two[b])
        product = nn(jnp.concatenate(split2(score), 1), tiled) * cross[trows]
        high, low = split2(product)
        direct = weights[trows, HEADS:]
        dw = by_channel(w_two[b]) * direct + nt(high, gather) + nt(low, gather)
        weight = weights[trows, :HEADS]
        wdw = weight * dw
        part = [wdw[c * BLK : (c + 1) * BLK] for c in range(CH)]
        own = jnp.concatenate(
            [sum(jnp.where(group[c] == g, part[c], 0.0) for c in range(CH)) for g in range(GR)], 0
        )
        score_grad[trows] = weight * (dw - by_channel(own))

    def turn(x):
        return jnp.concatenate([x, jnp.zeros((x.shape[0], 128 - HEADS), F32)], 1).T[:HEADS]

    def outer(left, right):
        both = nt(jnp.concatenate(split2(right), 0), left)
        return both[:HEADS] + both[HEADS:]

    score_turned[...] = turn(score_grad[...])
    ones = outer(tok_t[...], score_turned[...])
    copies[6].wait()
    twos = outer(agg_t[...], turn(jnp.concatenate(s_two, 0)))
    grads = jnp.concatenate([ones, twos], 0)
    copies[7].wait()
    copies[8].wait()
    started = [
        pltpu.make_async_copy(grad, value_grad, sems.at[9]),
        pltpu.make_async_copy(score_turned, score_grad_h, sems.at[10]),
    ]
    for c in started:
        c.start()
    lines = []
    for k, weight in enumerate((w_key, w_key_two)):
        high, low = split2(grads[k * HEADS : (k + 1) * HEADS])
        out = nn(jnp.concatenate([high, low], 0), weight[...])
        out = (out[:HEADS] + out[HEADS:]) * heads.astype(F32)
        lines.append(jnp.sum(out, 0, keepdims=True) * SCALE)
    quarters = jnp.concatenate(
        [line[:, k * 256 : (k + 1) * 256] for line in lines for k in range(4)], 0
    )
    left = (lax.broadcasted_iota(jnp.int32, (8, D), 1) & 64) == 0
    even, odd = [], []
    for k in range(2):
        one, two = grads[16 * k : 16 * k + 8], grads[16 * k + 8 : 16 * k + 16]
        even.append(jnp.where(left, one, jnp.concatenate([two[:, D - 64 :], two[:, : D - 64]], 1)))
        odd.append(jnp.where(left, jnp.concatenate([one[:, 64:], one[:, :64]], 1), two))
    mine = core[0]
    here = [jnp.where(mine == 0, x, y) for x, y in zip(even, odd)]
    away = [jnp.where(mine == 0, y, x) for x, y in zip(even, odd)]

    def small(pair, k):
        lanes = slice(k * 128, (k + 1) * 128)
        return jnp.concatenate([pair[0][:, lanes], pair[1][:, lanes], quarters], 1)

    for k in range(0, 8, 4):
        out = nn(peer_rows(tok_t, k, 1 - mine), grad[...])
        for i in range(4):
            extra[k + i] = small(here, k + i)
            other = small(away, k + i)
            for half in range(2):
                part = out[64 * i : 64 * (i + 1), half * 512 : (half + 1) * 512]
                send[8 * half + k + i] = jnp.concatenate([part, other], 0).astype(BF16)
    started.append(pltpu.make_async_copy(send, send_h, sems.at[11]))
    started.append(pltpu.make_async_copy(extra, extra_h, sems.at[13]))
    for c in started[-2:]:
        c.start()
    for c in started:
        c.wait()


def peer_rows(tok_t, k, side):
    return jnp.concatenate(
        [tok_t[pl.ds(pl.multiple_of((2 * (k + i) + side) * 64, 64), 64), :] for i in range(4)], 0
    )


def keep_kernel(core, tok_t, value_grad, extra, keep):
    mine = core[0]
    for k in range(0, 8, 4):
        out = nn(peer_rows(tok_t, k, mine), value_grad[...])
        for i in range(4):
            for half in range(2):
                part = out[64 * i : 64 * (i + 1), half * 512 : (half + 1) * 512]
                keep[8 * half + k + i] = jnp.concatenate([part, extra[k + i]], 0)


def pair_kernel(keep, got, out):
    out[...] = (keep[...] + got[...].astype(F32)).astype(BF16)


def token_kernel(value_grad, score_grad, w_value, fold_one, out):
    grad = nt(value_grad[...], w_value[...]) + folded_back(score_grad[...].T, fold_one[...])
    out[...] = grad.astype(BF16).reshape(CH, BLK, D)


def rows_kernel(got, out):
    total = got[0].astype(F32)
    for k in range(1, 16):
        total = total + got[k].astype(F32)
    for z in range(8):
        out[z] = jnp.concatenate([total[8 * z : 8 * z + 8], total[64:]], 1).astype(BF16)


def chans_kernel(got, rows, extra):
    total = got[0].astype(F32)
    for k in range(1, 8):
        total = total + got[k].astype(F32)
    own = total[:, :512].astype(BF16)
    for c in range(16):
        rows[c] = own
    extra[...] = total[:, 512:]


def last_kernel(got, out):
    for r in range(8):
        for half in range(2):
            out[8 * r : 8 * r + 8, half * 512 : (half + 1) * 512] = got[2 * r + half].astype(F32)


def small_kernel(extra, query_one, query_two, grad_key, grad_key_two, line_one, line_two):
    x = extra[...]
    grads = jnp.concatenate([x[:, k * 64 : (k + 1) * 64] for k in range(4)], 0)
    grads = jnp.concatenate([grads, jnp.zeros((96, 64), F32)], 0)
    turned = jnp.concatenate([grads, jnp.zeros((128, 64), F32)], 1).T[:64]
    heads3 = spread(3)
    for k, (query, out) in enumerate(((query_one, grad_key), (query_two, grad_key_two))):
        part = turned[:, k * HEADS : (k + 1) * HEADS]
        out[...] = nn(jnp.concatenate(split3(part), 1), heads3) * (query[...] * SCALE)
    for k in range(4):
        cols = slice(k * 256, (k + 1) * 256)
        line_one[:, cols] = x[k : k + 1, 256:]
        line_two[:, cols] = x[4 + k : 5 + k, 256:]


def shape(dims, dtype):
    return jax.ShapeDtypeStruct(dims, dtype)


SMEM = pl.BlockSpec(memory_space=pltpu.SMEM)


def whole(dims):
    return pl.BlockSpec(dims, lambda i: (0,) * len(dims))


def call(kernel, out_shape, flops, nbytes, limit=60, **kw):
    return pl.pallas_call(
        kernel,
        out_shape=out_shape,
        compiler_params=pltpu.CompilerParams(vmem_limit_bytes=int(limit * MIB)),
        cost_estimate=pl.CostEstimate(flops=flops, bytes_accessed=nbytes, transcendentals=0),
        **kw,
    )


def shards(tokens, table, w_key, w_value, query_one, w_key_two, query_two, cotangent):
    query_one, query_two = query_one.reshape(1, D), query_two.reshape(1, D)
    vmem = pl.BlockSpec(memory_space=pltpu.VMEM)
    hbm = pl.BlockSpec(memory_space=pltpu.HBM)
    tiled = call(
        tile_kernel,
        shape((16, ROWS // 16, D), BF16),
        10**4,
        10**6,
    )(cotangent)
    cot = lax.all_to_all(tiled, "chan", 0, 0, tiled=True).reshape(ROWS, D)
    full = whole((D, D))
    by_rows = lambda n, w: pl.BlockSpec((n, w), lambda i: (i, 0))
    by_cols = lambda n: pl.BlockSpec((D, n), lambda i: (0, i))
    token_spec = pl.BlockSpec((CH, BLK, D), lambda i: (0, i, 0))
    values, weights, agg, agg_t, tok_t, scores_two, fold_one, fold_two, cross = call(
        forward_kernel,
        (
            shape((NB * TOK, D), F32),
            shape((NB * TOK, HEADS), F32),
            shape((NB * AGG, D), BF16),
            shape((D, NB * AGG), BF16),
            shape((D, NB * TOK), BF16),
            shape((NB * AGG, HEADS), F32),
            shape((D, 3 * HEADS), BF16),
            shape((D, 3 * HEADS), BF16),
            shape((NB * TOK, PAIRS), F32),
        ),
        4 * 10**9,
        16 * 10**6,
        grid=(NB,),
        in_specs=[SMEM, token_spec, full, full, full, whole((1, D)), whole((1, D))],
        out_specs=(
            by_rows(TOK, D),
            by_rows(TOK, HEADS),
            by_rows(AGG, D),
            by_cols(AGG),
            by_cols(TOK),
            by_rows(AGG, HEADS),
            whole((D, 3 * HEADS)),
            whole((D, 3 * HEADS)),
            by_rows(TOK, PAIRS),
        ),
        scratch_shapes=[pltpu.VMEM((2, D, PAIRS), BF16)],
    )(table, tokens, w_value, w_key, w_key_two, query_one, query_two)
    pair_two, stats = call(
        stats_kernel,
        (shape((NB * AGG, 2 * HEADS), F32), shape((16, 48, 128), F32)),
        10**9,
        2 * 10**6,
    )(agg, cot, scores_two)
    stats, values, weights = lax.optimization_barrier((stats, values, weights))
    stats = lax.all_to_all(stats, "chan", 0, 0, tiled=True)
    core = lax.rem(lax.axis_index("patch"), 2).astype(jnp.int32).reshape(1)
    weights = call(
        pre_kernel, shape((NB * TOK, 2 * HEADS), F32), 10**9, 5 * 10**6
    )(values, cot, weights)
    totals = call(total_kernel, shape((48, 128), F32), 10**6, 10**6, 4)(stats)
    fetched = (cot, pair_two, weights, fold_two, tok_t, cross, agg_t, w_key, w_key_two)
    value_grad, score_grad, send, extra = call(
        back_kernel,
        (
            shape((NB * TOK, D), BF16),
            shape((HEADS, NB * TOK), F32),
            shape((16, SLAB, 512), BF16),
            shape((8, 8, 512), F32),
        ),
        4 * 10**9,
        16 * 10**6,
        53.7,
        in_specs=[SMEM, SMEM] + [hbm] * (1 + len(fetched)),
        out_specs=(hbm, hbm, hbm, hbm),
        scratch_shapes=[pltpu.VMEM(x.shape, x.dtype) for x in (totals,) + fetched]
        + [
            pltpu.VMEM((NB * TOK, D), BF16),
            pltpu.VMEM((16, SLAB, 512), BF16),
            pltpu.VMEM((NB * TOK, HEADS), F32),
            pltpu.VMEM((HEADS, NB * TOK), F32),
            pltpu.VMEM((8, 8, 512), F32),
            pltpu.SemaphoreType.DMA((14,)),
        ],
    )(table, core, totals, *fetched)
    got = lax.ppermute(send, "patch", [(i, i ^ 1) for i in range(16)])
    keep = call(
        keep_kernel,
        shape((16, SLAB, 512), F32),
        10**9,
        5 * 10**6,
        16,
        in_specs=[SMEM, vmem, vmem, vmem],
    )(core, tok_t, value_grad, extra)
    slabs = pl.BlockSpec((4, SLAB, 512), lambda i: (i, 0, 0))
    pairs = call(
        pair_kernel,
        shape((16, SLAB, 512), BF16),
        10**6,
        5 * 10**6,
        12,
        grid=(4,),
        in_specs=[slabs, slabs],
        out_specs=slabs,
    )(keep, got)
    planes = [
        [(2 * z + h) * 16 + 2 * k + core_bit for h in range(2) for k in range(8)]
        for z in range(8)
        for core_bit in range(2)
    ]
    got = lax.all_to_all(
        pairs, ("chan", "patch"), 0, 0, tiled=True, axis_index_groups=planes
    )
    token_grad = call(
        token_kernel,
        shape((CH, ROWS, D), BF16),
        2 * 10**9,
        6 * 10**6,
        24,
        grid=(NB,),
        in_specs=[
            by_rows(TOK, D),
            pl.BlockSpec((HEADS, TOK), lambda i: (0, i)),
            full,
            whole((D, 3 * HEADS)),
        ],
        out_specs=token_spec,
    )(value_grad, score_grad, w_value, fold_one)
    rows = call(rows_kernel, shape((8, 8, D), BF16), 10**6, 2 * 10**6, 8)(got)
    same_half = [[2 * z + h for z in range(8)] for h in range(2)]
    rows = lax.all_to_all(rows, "chan", 0, 0, tiled=True, axis_index_groups=same_half)
    rows, extra = call(
        chans_kernel, (shape((16, 8, 512), BF16), shape((8, 512), F32)), 10**6, 10**6, 8
    )(rows)
    rows = lax.all_to_all(rows, "chan", 0, 0, tiled=True)
    grad_value = call(last_kernel, shape((64, D), F32), 10**6, 10**6, 8)(rows)
    grad_key, grad_key_two, line_one, line_two = call(
        small_kernel,
        (shape((64, D), F32), shape((64, D), F32), shape((1, D), F32), shape((1, D), F32)),
        10**8,
        10**6,
        8,
    )(extra, query_one, query_two)
    return (
        token_grad,
        grad_key,
        grad_value,
        grad_key_two,
        line_one.reshape(D),
        line_two.reshape(D),
    )


def solution(mesh):
    return jax.shard_map(
        shards,
        mesh=mesh,
        in_specs=(
            P("chan", "patch", None),
            P("chan"),
            P(),
            P(),
            P(),
            P(),
            P(),
            P("patch", "chan", None),
        ),
        out_specs=(
            P("chan", "patch", None),
            P("patch", None),
            P("patch", None),
            P("patch", None),
            P(),
            P(),
        ),
        check_vma=False,
    )
```
